32 devices in a mesh: group: 2 (over x), head: 16 (over z, y, core).
Axes of the slice: x: 2, y: 2, z: 4, core: 2. Of those that a mesh axis runs over, the one named last changes fastest.
Arguments:
- q_heads: bfloat16 [64, 24576], P('group', 'head'), parts along dimension 0, may hold values from -16 to 16
- w_absorb: bfloat16 [128, 128, 512], P('head'), may hold values from -0.5 to 0.5
- w_value: bfloat16 [128, 512, 128], P('head'), may hold values from -0.25 to 0.25
- w_out: bfloat16 [16384, 7168], P('head'), may hold values from -0.1875 to 0.1875
- latent_cache: bfloat16 [64, 128, 576], P(('group', 'head')), parts along dimension 0, may hold values from -6 to 6
- ctx_blocks: int32 [16], P('group'), parts along dimension 0, may hold values from 1 to 8, 32 in all
- block_table: int32 [16, 8], P('group'), parts along dimension 0, may hold values from 0 to 31, as said below
- owner: int32 [16], P('group'), parts along dimension 0, may hold values from 0 to 15, as said below
Outputs:
- attended: bfloat16 [128, 7168], P(('group', 'head')), parts along dimension 0
The draws below stay inside these ranges and needn't reach their ends.
There are 2 independent parts, one for each index of `group`. The reference program is written for one: setup_inputs(seed, part) draws one part's arguments, and reference() takes and returns one part's arrays. A program takes and returns all parts, laid end to end along the dimension named above; an argument that names none is the same for every part. Nothing has to cross between parts.
Inputs may be any that keep to these rules, and one draw needn't show every extreme that they name: `block_table`: the entries of a row are distinct, every cache block appears exactly twice in the table; entries at or beyond a request's length are not used. `owner`: requests of a group have distinct decode devices.
All inputs are finite; a program needn't handle non-finite values.
Results may differ from the reference program's by a relative error of at most 0.0085.
Values may be sent and summed in bfloat16 or wider, within the bound.
No kernel may reach another device: no remote copies, remote signals or barrier semaphores. Data moves between devices by JAX's collectives and lax.ppermute only.
A program may use at most 128 MiB of HBM per device.

```python
import math
import jax
import jax.numpy as jnp
import numpy as np
from jax import lax

H = 128
KV_RANK = 512
ROPE = 64
NOPE = 128
VHEAD = 128
D = 7168
BLOCK = 128
STEPS = 4
MAXB = 8
NB = 32
REQ = 8
ROWS = 32
N_HEAD = 16


def draw_q_heads(key, part):
    key = jax.random.fold_in(key, 11)
    first = jax.random.fold_in(key, 0)
    full = jnp.clip(jax.random.normal(first, (ROWS, H, NOPE + ROPE), jnp.float32), -6.0, 6.0)
    return full.reshape(ROWS, H * (NOPE + ROPE)).astype(jnp.bfloat16)


def draw_latent_cache(key, part):
    key = jax.random.fold_in(key, 23)
    first = jax.random.fold_in(key, 0)
    full = jnp.clip(jax.random.normal(first, (NB, BLOCK, KV_RANK + ROPE), jnp.float32), -6.0, 6.0)
    return full.astype(jnp.bfloat16)


def draw_block_table(key, part):
    key = jax.random.fold_in(key, 37)
    first, second = jax.random.split(key, 2)
    earlier = jax.random.permutation(first, NB)
    later = jax.random.permutation(second, NB)
    return jnp.concatenate([earlier, later]).reshape(REQ, MAXB).astype(jnp.int32)


def draw_owner(key, part):
    key = jax.random.fold_in(key, 41)
    first, second = jax.random.split(key, 2)
    inner = jax.random.permutation(first, N_HEAD - 2)[:REQ - 2] + 1
    chosen = jnp.concatenate([jnp.array([0, N_HEAD - 1], dtype=jnp.int32), inner.astype(jnp.int32)])
    return jax.random.permutation(second, chosen).astype(jnp.int32)


def levels(own_key, dims, shards, low, high):
    def one(axis_at, blocks):
        steps = jax.random.uniform(jax.random.fold_in(jax.random.fold_in(own_key, 6), axis_at), (blocks,), jnp.float32, low / len(shards), high / len(shards))
        return jnp.repeat(jnp.exp(steps), dims[axis_at] // blocks).reshape((-1,) + (1,) * (len(dims) - axis_at - 1))

    factor_of = one(*shards[0])
    for cut in shards[1:]:
        factor_of = factor_of * one(*cut)
    return factor_of


def split_up(number_of, total, reach, slope):
    portions = [(1 << 20) // math.isqrt(grade ** slope) + 1 for grade in range(2, number_of + 1)]
    rest, counts = total - reach - (number_of - 1), [1] * (number_of - 1)
    while rest > 0:
        movable = [i for i in range(number_of - 1) if counts[i] < reach]
        pool, remaining = sum([portions[i] for i in movable]), rest
        for i in movable:
            extra = min(reach - counts[i], max(1, remaining * portions[i] // pool), rest)
            counts[i] = counts[i] + extra
            rest = rest - extra
    return np.array([reach] + counts)


def ragged_sizes(rng, number_of, total, limit, lean):
    if number_of == 2:
        one = jax.random.randint(rng, (), max(1, total - limit), min(limit, total - 1) + 1)
        return jnp.stack([one, total - one])
    sizes = jnp.asarray(split_up(number_of, total, limit, lean), jnp.int32)
    couples = (number_of - 1) // 2
    source_of, taker = sizes[1:1 + 2 * couples:2], sizes[2:2 + 2 * couples:2]
    margin = jnp.minimum(source_of - 1, limit - taker)
    passed = jax.random.randint(jax.random.fold_in(rng, 1), (couples,), 0, 1 << 20) % (margin + 1)
    sizes = sizes.at[1:1 + 2 * couples:2].set(source_of - passed).at[2:2 + 2 * couples:2].set(taker + passed)
    return sizes[jax.random.permutation(jax.random.fold_in(rng, 2), number_of)]


def scatter_about(stream_key, shape, deviation, reach, cuts=(), kind=jnp.bfloat16):
    loudness = levels(stream_key, shape, cuts, -0.22, 0.18) if cuts else 1.0
    values = jax.random.normal(stream_key, shape, jnp.float32) * deviation * loudness
    return jnp.minimum(jnp.maximum(values, -reach), reach).astype(kind)


def setup_inputs(seed: int = 0, part: int = 0) -> dict:
    streams_of = jax.random.split(jax.random.key(seed), 9)
    part_keys = jax.random.split(jax.random.fold_in(streams_of[8], part), 9)
    q_heads = draw_q_heads(jax.random.fold_in(jax.random.fold_in(streams_of[8], part), 71), part)
    w_absorb = scatter_about(streams_of[1], (H, NOPE, KV_RANK), NOPE ** -0.5, 0.5, ((0, 16),))
    w_value = scatter_about(streams_of[2], (H, KV_RANK, VHEAD), KV_RANK ** -0.5, 0.25, ((0, 16),))
    w_out = scatter_about(streams_of[3], (H * VHEAD, D), (H * VHEAD // 16) ** -0.5, 0.1875, ((0, 16),))
    latent_cache = draw_latent_cache(jax.random.fold_in(jax.random.fold_in(streams_of[8], part), 71), part)
    ctx_blocks = ragged_sizes(part_keys[5], REQ, NB, MAXB, 2).astype(jnp.int32)
    block_table = draw_block_table(jax.random.fold_in(jax.random.fold_in(streams_of[8], part), 71), part)
    owner = draw_owner(jax.random.fold_in(jax.random.fold_in(streams_of[8], part), 71), part)
    return dict(q_heads=q_heads, w_absorb=w_absorb, w_value=w_value, w_out=w_out, latent_cache=latent_cache, ctx_blocks=ctx_blocks, block_table=block_table, owner=owner)


def reference(q_heads, w_absorb, w_value, w_out, latent_cache, ctx_blocks, block_table, owner):
    row_width = KV_RANK + ROPE
    score_scale = (NOPE + ROPE) ** -0.5
    queries = q_heads.reshape(ROWS, H, NOPE + ROPE)
    q_nope = queries[:, :, :NOPE].astype(jnp.float32)
    q_latent = jnp.einsum("rhn,hnc->rhc", q_nope, w_absorb.astype(jnp.float32)).astype(jnp.bfloat16)
    q_full = jnp.concatenate([q_latent, queries[:, :, NOPE:]], axis=2)
    per_request = q_full.reshape(REQ, STEPS, H, row_width)
    offsets = jnp.arange(MAXB * BLOCK, dtype=jnp.int32)
    step_ids = jnp.arange(STEPS, dtype=jnp.int32)

    def attend(members):
        request_queries, table_row, length = members
        key_rows = latent_cache[table_row.astype(jnp.int32)].reshape(MAXB * BLOCK, row_width)
        scores = jnp.einsum("shc,tc->sht", request_queries.astype(jnp.float32), key_rows.astype(jnp.float32)) * score_scale
        limits = length * BLOCK - (STEPS - 1 - step_ids)
        visible = offsets[None, :] < limits[:, None]
        scores = jnp.where(visible[:, None, :], scores, -jnp.inf)
        weights = jax.nn.softmax(scores, axis=-1).astype(jnp.bfloat16)
        latent_out = jnp.einsum("sht,tc->shc", weights.astype(jnp.float32), key_rows[:, :KV_RANK].astype(jnp.float32))
        return latent_out.astype(jnp.bfloat16)

    latent_out = lax.map(attend, (per_request, block_table, ctx_blocks))
    value_out = jnp.einsum("rshc,hcv->rshv", latent_out.astype(jnp.float32), w_value.astype(jnp.float32)).astype(jnp.bfloat16)
    head_out = value_out.reshape(ROWS, H * VHEAD)
    projected = jnp.dot(head_out, w_out, preferred_element_type=jnp.float32)
    slot_rows = (owner[:, None] * STEPS + step_ids[None, :]).reshape(ROWS).astype(jnp.int32)
    placed = jnp.zeros((N_HEAD * STEPS, D), jnp.float32).at[slot_rows].set(projected)
    return placed.astype(jnp.bfloat16)
```

```python
import functools

import jax
import jax.numpy as jnp
import numpy as np
from jax import lax
from jax.experimental import pallas as pl
from jax.experimental.pallas import tpu as pltpu
from jax.sharding import PartitionSpec as P

OUT_TILE = 1024
LANES = 128


def ring_of(chips):
    if chips == 8:
        return [0, 2, 4, 6, 7, 5, 3, 1]
    return list(range(chips))


def gather_pieces(keys, chips):
    ring = ring_of(chips)
    up = [
        (ring[i] * 2 + core, ring[(i + 1) % chips] * 2 + core)
        for i in range(chips)
        for core in range(2)
    ]
    down = [(b, a) for a, b in up]
    swap = [(i, i ^ 1) for i in range(2 * chips)]
    half = keys.shape[0] // 2
    lower, upper = keys[:half], keys[half:]
    ups, downs = [lower, upper], [lower, upper]
    pieces, places = [lower, upper], [(0, 0), (0, 1)]
    for hop in range(1, chips // 2 + 1):
        last = hop == chips // 2
        for part in range(2):
            if not last or part == 0:
                ups[part] = lax.ppermute(ups[part], "head", up)
                pieces.append(ups[part])
                places.append((-hop, part))
            if not last or part == 1:
                downs[part] = lax.ppermute(downs[part], "head", down)
                pieces.append(downs[part])
                places.append((hop, part))
    own = len(pieces)
    pieces = pieces + [lax.ppermute(p, "head", swap) for p in pieces]
    places = [(hop, part, 0) for hop, part in places] + [(hop, part, 1) for hop, part in places]
    return pieces, places


def slots_by_device(places, chips, half):
    ring = ring_of(chips)
    position = {chip: i for i, chip in enumerate(ring)}
    table = np.zeros((2 * chips, 4 * chips * half), np.int32)
    for device in range(2 * chips):
        for index, (hop, part, flip) in enumerate(places):
            chip = ring[(position[device // 2] + hop) % chips]
            source = chip * 2 + (device % 2 ^ flip)
            for i in range(half):
                table[device, (source * 2 + part) * half + i] = index * half + i
    return table


def attend_kernel(
    piece_count, half, heads, steps, scale,
    me_ref, length_ref, table_ref, owner_ref, slot_ref, query_ref, value_ref, out_w_ref, *rest,
):
    pieces = rest[:piece_count]
    (away_ref, keep_ref, cache, weight, scores, top, total, latent, head_rows,
     use_request, use_block, use_last, cache_sems, weight_sems) = rest[piece_count:]
    requests, row_block, _ = query_ref.shape
    kv_rank = value_ref.shape[1]
    v_width = value_ref.shape[2]
    block_rows = cache.shape[2]
    rows = requests * steps
    tiles, _, tile = weight.shape
    uses = scores.shape[0]

    piece_copies = [
        pltpu.make_async_copy(p, cache.at[pl.ds(i * half, half)], cache_sems.at[i])
        for i, p in enumerate(pieces)
    ]
    for copy in piece_copies:
        copy.start()
    weight_copies = [
        pltpu.make_async_copy(out_w_ref.at[:, pl.ds(i * tile, tile)], weight.at[i], weight_sems.at[i])
        for i in range(tiles)
    ]
    for copy in weight_copies:
        copy.start()

    def list_request(r, at):
        count = length_ref[r]

        def list_block(j, _):
            use_request[at + j] = r
            use_block[at + j] = slot_ref[table_ref[r, j]]
            use_last[at + j] = (j == count - 1).astype(jnp.int32)
            return 0

        lax.fori_loop(0, count, list_block, 0)
        return at + count

    lax.fori_loop(0, requests, list_request, 0)

    top[...] = jnp.full_like(top, -jnp.inf)
    total[...] = jnp.zeros_like(total)
    latent[...] = jnp.zeros_like(latent)
    column = lax.broadcasted_iota(jnp.int32, (row_block, block_rows), 1)
    step = lax.broadcasted_iota(jnp.int32, (row_block, block_rows), 0) // heads
    hidden = steps - 1 - step
    for copy in piece_copies:
        copy.wait()

    def score(u, _):
        r = use_request[u]
        s = jnp.dot(query_ref[r], cache[use_block[u]], preferred_element_type=jnp.float32) * scale
        s = jnp.where(column + hidden * use_last[u] < block_rows, s, -jnp.inf)
        scores[u] = s
        top[r] = jnp.maximum(top[r], s)
        return 0

    lax.fori_loop(0, uses, score, 0, unroll=4)

    def peak(r, _):
        top[r] = jnp.broadcast_to(jnp.max(top[r], axis=1, keepdims=True), (row_block, block_rows))
        return 0

    lax.fori_loop(0, requests, peak, 0, unroll=4)

    def gather(u, _):
        r = use_request[u]
        p = jnp.exp(scores[u] - top[r])
        total[r] += p
        mixed = lax.dot_general(
            p.astype(jnp.bfloat16),
            cache[use_block[u], :kv_rank],
            (((1,), (1,)), ((), ())),
            preferred_element_type=jnp.float32,
        )
        at = pl.ds(pl.multiple_of(r * row_block, row_block), row_block)
        for c in range(kv_rank // LANES):
            latent[c, at] += mixed[:, c * LANES : (c + 1) * LANES]
        return 0

    lax.fori_loop(0, uses, gather, 0, unroll=4)

    def normalise(r, _):
        at = pl.ds(pl.multiple_of(r * row_block, row_block), row_block)
        norm = jnp.sum(total[r], axis=1, keepdims=True)
        for c in range(kv_rank // LANES):
            latent[c, at] = latent[c, at] / norm
        return 0

    lax.fori_loop(0, requests, normalise, 0, unroll=4)

    for h in range(heads):
        mine = jnp.concatenate(
            [latent[c, pl.ds(h, rows, stride=heads)] for c in range(kv_rank // LANES)], axis=1
        ).astype(jnp.bfloat16)
        head_rows[:, h * v_width : (h + 1) * v_width] = jnp.dot(
            mine, value_ref[h], preferred_element_type=jnp.float32
        ).astype(jnp.bfloat16)

    half_rows = away_ref.shape[0]
    chips = half_rows // steps
    me = me_ref[0]
    target = lax.broadcasted_iota(jnp.int32, (2 * half_rows, rows), 0)
    origin = lax.broadcasted_iota(jnp.int32, (2 * half_rows, rows), 1)

    def place(r, picked):
        apart = owner_ref[r] ^ me
        order = (apart & 1) * chips + ((apart >> 1) & 1) * (chips // 2) + (apart >> 2)
        shifted = origin - r * steps
        hit = (target - order * steps == shifted) & (shifted >= 0) & (shifted < steps)
        return jnp.where(hit, 1.0, picked)

    picker = lax.fori_loop(0, requests, place, jnp.zeros((2 * half_rows, rows), jnp.float32))
    placed = jnp.dot(
        picker.astype(jnp.bfloat16), head_rows[...], preferred_element_type=jnp.float32
    ).astype(jnp.bfloat16)
    for i in range(tiles):
        weight_copies[i].wait()
        result = jnp.dot(placed, weight[i], preferred_element_type=jnp.float32).astype(jnp.bfloat16)
        keep_ref[:, i * tile : (i + 1) * tile] = result[:half_rows]
        away_ref[:, i * tile : (i + 1) * tile] = result[half_rows:]


def local(q_heads, w_absorb, w_value, w_out, latent_cache, ctx_blocks, block_table, owner):
    heads, nope_width, kv_rank = w_absorb.shape
    row_count = q_heads.shape[0]
    head_width = q_heads.shape[1] // heads
    requests, max_blocks = block_table.shape
    steps = row_count // requests
    devices = lax.axis_size("head")
    chips = devices // 2
    blocks_here, block_rows, row_width = latent_cache.shape
    half = blocks_here // 2
    width = w_out.shape[1]
    v_width = w_value.shape[2]
    me = lax.axis_index("head").astype(jnp.int32)

    pieces, places = gather_pieces(jnp.swapaxes(latent_cache, 1, 2), chips)
    slots = jnp.asarray(slots_by_device(places, chips, half))[me]

    queries = q_heads.reshape(row_count, heads, head_width)
    q_latent = jnp.einsum(
        "rhn,hnc->rhc", queries[:, :, :nope_width], w_absorb, preferred_element_type=jnp.float32
    ).astype(jnp.bfloat16)
    q_full = jnp.concatenate([q_latent, queries[:, :, nope_width:]], axis=2)
    q_full = q_full.reshape(requests, steps * heads, row_width)

    uses = blocks_here * devices
    row_block = steps * heads
    tiles = width // OUT_TILE
    smem = pl.BlockSpec(memory_space=pltpu.SMEM)
    vmem = pl.BlockSpec(memory_space=pltpu.VMEM)
    anywhere = pl.BlockSpec(memory_space=pl.ANY)
    part = jax.ShapeDtypeStruct((chips * steps, width), jnp.bfloat16)
    away, keep = pl.pallas_call(
        functools.partial(
            attend_kernel, len(pieces), half, heads, steps, float(head_width) ** -0.5
        ),
        out_shape=(part, part),
        in_specs=[smem] * 5 + [vmem] * 2 + [anywhere] * (1 + len(pieces)),
        out_specs=(vmem, vmem),
        scratch_shapes=[
            pltpu.VMEM((uses, row_width, block_rows), jnp.bfloat16),
            pltpu.VMEM((tiles, w_out.shape[0], OUT_TILE), jnp.bfloat16),
            pltpu.VMEM((uses, row_block, block_rows), jnp.float32),
            pltpu.VMEM((requests, row_block, block_rows), jnp.float32),
            pltpu.VMEM((requests, row_block, block_rows), jnp.float32),
            pltpu.VMEM((kv_rank // LANES, requests * row_block, LANES), jnp.float32),
            pltpu.VMEM((row_count, heads * v_width), jnp.bfloat16),
            pltpu.SMEM((uses,), jnp.int32),
            pltpu.SMEM((uses,), jnp.int32),
            pltpu.SMEM((uses,), jnp.int32),
            pltpu.SemaphoreType.DMA((len(pieces),)),
            pltpu.SemaphoreType.DMA((tiles,)),
        ],
        compiler_params=pltpu.CompilerParams(vmem_limit_bytes=48 * 1024 * 1024),
        name="attend_and_project",
    )(me.reshape(1), ctx_blocks, block_table, owner, slots, q_full, w_value, w_out, *pieces)

    def exchange(x, distance):
        return lax.ppermute(x, "head", [(i, i ^ distance) for i in range(devices)])

    def add(x, *others):
        total = x.astype(jnp.float32)
        for other in others:
            total = total + other.astype(jnp.float32)
        return total.astype(jnp.bfloat16)

    both = add(keep, exchange(away, 1))
    middle = both.shape[0] // 2
    line = add(both[:middle], exchange(both[middle:], 2))
    received = [
        exchange(line[k * steps : (k + 1) * steps], 4 * k) for k in range(1, chips // 2)
    ]
    return add(line[:steps], *received)


def solution(mesh):
    return jax.shard_map(
        local,
        mesh=mesh,
        in_specs=(
            P("group", "head"),
            P("head", None, None),
            P("head", None, None),
            P("head", None),
            P(("group", "head"), None, None),
            P("group"),
            P("group", None),
            P("group"),
        ),
        out_specs=P(("group", "head"), None),
        check_vma=False,
    )
```

```python
import functools

import jax
import jax.numpy as jnp
import numpy as np
from jax import lax
from jax.experimental import pallas as pl
from jax.experimental.pallas import tpu as pltpu
from jax.sharding import PartitionSpec as P

OUT_TILE = 1024
LANES = 128
UNROLL = 4
EMPTY = -1e30


def ring_of(chips):
    if chips == 8:
        return [0, 2, 4, 6, 7, 5, 3, 1]
    return list(range(chips))


def ring_places(chips):
    places = [(0, 0), (0, 1)]
    for hop in range(1, chips // 2 + 1):
        last = hop == chips // 2
        places += [(-hop, 0)] if last else [(-hop, 0), (hop, 0), (-hop, 1)]
        places += [(hop, 1)]
    return places


def slots_by_device(chips, half):
    ring = ring_of(chips)
    position = {chip: i for i, chip in enumerate(ring)}
    table = np.full((2 * chips, 4 * chips * half), -1, np.int32)
    for device in range(2 * chips):
        for index, (hop, part) in enumerate(ring_places(chips)):
            source = ring[(position[device // 2] + hop) % chips] * 2 + device % 2
            for i in range(half):
                table[device, (source * 2 + part) * half + i] = index * half + i
    return table


def query_kernel(heads, query_ref, absorb_ref, out_ref, ordered):
    rows = query_ref.shape[0]
    nope = absorb_ref.shape[1]
    head_width = query_ref.shape[1] // heads
    rope = head_width - nope
    kv_rank = absorb_ref.shape[2]
    for h in range(heads):
        own = query_ref[:, h * head_width : (h + 1) * head_width]
        latent = jnp.dot(own[:, :nope], absorb_ref[h], preferred_element_type=jnp.float32)
        turned = jnp.concatenate(
            [own[:, nope:].astype(jnp.float32), jnp.zeros((rows, LANES - rope), jnp.float32)], axis=1
        )
        at = pl.ds(h, rows, stride=heads)
        for c in range(kv_rank // LANES):
            ordered[c, at] = latent[:, c * LANES : (c + 1) * LANES]
        ordered[kv_rank // LANES, at] = turned
    for c in range(kv_rank // LANES):
        out_ref[:, c * LANES : (c + 1) * LANES] = ordered[c].astype(jnp.bfloat16)
    out_ref[:, kv_rank:] = ordered[kv_rank // LANES, :, :rope].astype(jnp.bfloat16)


def attend_kernel(
    piece_count, first_slot, heads, steps, max_blocks, kv_rank, scale,
    info_ref, mine_ref, theirs_ref, *rest,
):
    pieces = rest[:piece_count]
    (out_ref, lse_ref, away_ref, queries, cache, scores, top, total, latent,
     use_request, use_block, use_last, cache_sems) = rest[piece_count:]
    requests = top.shape[0] - 1
    row_block = queries.shape[1] // 2
    both = 2 * row_block
    block_rows = cache.shape[2]
    half = cache.shape[0] // piece_count
    slot_at = requests * (max_blocks + 2)

    copies = [
        pltpu.make_async_copy(p, cache.at[pl.ds(i * half, half)], cache_sems.at[i])
        for i, p in enumerate(pieces)
    ]
    for copy in copies:
        copy.start()

    def list_request(r, at):
        count = info_ref[r]

        def list_block(j, at):
            slot = info_ref[slot_at + info_ref[requests * 2 + r * max_blocks + j]] - first_slot
            here = (slot >= 0) & (slot < cache.shape[0])

            @pl.when(here)
            def _():
                use_request[at] = r
                use_block[at] = slot
                use_last[at] = (j == count - 1).astype(jnp.int32)

            return at + here.astype(jnp.int32)

        return lax.fori_loop(0, count, list_block, at)

    uses = lax.fori_loop(0, requests, list_request, 0)
    for i in range(UNROLL):
        use_request[uses + i] = requests
        use_block[uses + i] = 0
        use_last[uses + i] = 0
    turns = (uses + UNROLL - 1) // UNROLL

    queries[:, :row_block] = mine_ref[...]
    queries[:, row_block:] = theirs_ref[...]
    top[...] = jnp.full_like(top, -jnp.inf)
    total[...] = jnp.zeros_like(total)
    latent[...] = jnp.zeros_like(latent)
    column = lax.broadcasted_iota(jnp.int32, (both, block_rows), 1)
    row = lax.broadcasted_iota(jnp.int32, (both, block_rows), 0)
    hidden = steps - 1 - (row % row_block) // heads
    for copy in copies:
        copy.wait()

    def score(turn, _):
        for i in range(UNROLL):
            u = turn * UNROLL + i
            r = use_request[u]
            s = jnp.dot(
                queries[jnp.minimum(r, requests - 1)], cache[use_block[u]],
                preferred_element_type=jnp.float32,
            ) * scale
            s = jnp.where(column + hidden * use_last[u] < block_rows, s, -jnp.inf)
            scores[u] = s
            top[r] = jnp.maximum(top[r], s)
        return 0

    lax.fori_loop(0, turns, score, 0)

    def peak(r, _):
        top[r] = jnp.broadcast_to(jnp.max(top[r], axis=1, keepdims=True), (both, block_rows))
        return 0

    lax.fori_loop(0, requests + 1, peak, 0)

    def mix(turn, _):
        for i in range(UNROLL):
            u = turn * UNROLL + i
            r = use_request[u]
            p = jnp.exp(scores[u] - top[r])
            total[r] += p
            latent[r] += lax.dot_general(
                p.astype(jnp.bfloat16),
                cache[use_block[u], :kv_rank],
                (((1,), (1,)), ((), ())),
                preferred_element_type=jnp.float32,
            )
        return 0

    lax.fori_loop(0, turns, mix, 0)

    lane = lax.broadcasted_iota(jnp.int32, (row_block, LANES), 1)

    def finish(r, _):
        at = pl.ds(pl.multiple_of(r * row_block, row_block), row_block)
        norm = jnp.sum(total[r], axis=1, keepdims=True)
        some = norm > 0
        safe = jnp.where(some, norm, 1.0)
        lse = jnp.where(some, top[r][:, :1] + jnp.log(safe), EMPTY)
        result = latent[r] / safe
        out_ref[at] = result[:row_block]
        lse_ref[at] = jnp.broadcast_to(lse[:row_block], (row_block, LANES))
        rest = lse[row_block:]
        high = rest.astype(jnp.bfloat16).astype(jnp.float32)
        middle = (rest - high).astype(jnp.bfloat16).astype(jnp.float32)
        low = rest - high - middle
        terms = jnp.where(lane == 0, high, jnp.where(lane == 1, middle, jnp.where(lane == 2, low, 0.0)))
        away_ref[at, :kv_rank] = result[row_block:].astype(jnp.bfloat16)
        away_ref[at, kv_rank:] = terms.astype(jnp.bfloat16)
        return 0

    lax.fori_loop(0, requests, finish, 0)


def project_kernel(
    stages, heads, steps, max_blocks, chips,
    info_ref, value_ref, out_w_ref, *rest,
):
    outs, lses, others = rest[:stages], rest[stages : 2 * stages], rest[2 * stages : 3 * stages]
    away_ref, keep_ref, latent, weight, head_rows, weight_sems = rest[3 * stages :]
    kv_rank, v_width = value_ref.shape[1:]
    rows = head_rows.shape[0]
    requests = rows // steps
    tiles, _, tile = weight.shape
    weight_copies = [
        pltpu.make_async_copy(out_w_ref.at[:, pl.ds(i * tile, tile)], weight.at[i], weight_sems.at[i])
        for i in range(tiles)
    ]
    for copy in weight_copies:
        copy.start()

    chunk = 64

    def merge(i, _):
        at = pl.ds(pl.multiple_of(i * chunk, chunk), chunk)
        parts = [(o[at], e[at][:, :1]) for o, e in zip(outs, lses)]
        for other in others:
            terms = jnp.sum(other[at, kv_rank:].astype(jnp.float32), axis=1, keepdims=True)
            parts.append((other[at, :kv_rank].astype(jnp.float32), terms))
        peak = functools.reduce(jnp.maximum, [e for _, e in parts])
        shares = [jnp.exp(e - peak) for _, e in parts]
        norm = functools.reduce(jnp.add, shares)
        whole = functools.reduce(jnp.add, [o * (w / norm) for (o, _), w in zip(parts, shares)])
        for c in range(kv_rank // LANES):
            latent[c, at] = whole[:, c * LANES : (c + 1) * LANES]
        return 0

    lax.fori_loop(0, rows * heads // chunk, merge, 0)

    for h in range(heads):
        mine = jnp.concatenate(
            [latent[c, pl.ds(h, rows, stride=heads)] for c in range(kv_rank // LANES)], axis=1
        ).astype(jnp.bfloat16)
        head_rows[:, h * v_width : (h + 1) * v_width] = jnp.dot(
            mine, value_ref[h], preferred_element_type=jnp.float32
        ).astype(jnp.bfloat16)

    half_rows = away_ref.shape[0]
    me = info_ref[info_ref.shape[0] - 1]
    target = lax.broadcasted_iota(jnp.int32, (2 * half_rows, rows), 0)
    origin = lax.broadcasted_iota(jnp.int32, (2 * half_rows, rows), 1)

    def place(r, picked):
        apart = info_ref[requests + r] ^ me
        order = (apart & 1) * chips + ((apart >> 1) & 1) * (chips // 2) + (apart >> 2)
        shifted = origin - r * steps
        hit = (target - order * steps == shifted) & (shifted >= 0) & (shifted < steps)
        return jnp.where(hit, 1.0, picked)

    picker = lax.fori_loop(0, requests, place, jnp.zeros((2 * half_rows, rows), jnp.float32))
    placed = jnp.dot(
        picker.astype(jnp.bfloat16), head_rows[...], preferred_element_type=jnp.float32
    ).astype(jnp.bfloat16)
    for i in range(tiles):
        weight_copies[i].wait()
        result = jnp.dot(placed, weight[i], preferred_element_type=jnp.float32).astype(jnp.bfloat16)
        keep_ref[:, i * tile : (i + 1) * tile] = result[:half_rows]
        away_ref[:, i * tile : (i + 1) * tile] = result[half_rows:]


def local(q_heads, w_absorb, w_value, w_out, latent_cache, ctx_blocks, block_table, owner):
    heads, _, kv_rank = w_absorb.shape
    row_count = q_heads.shape[0]
    head_width = q_heads.shape[1] // heads
    requests, max_blocks = block_table.shape
    steps = row_count // requests
    devices = lax.axis_size("head")
    chips = devices // 2
    blocks_here, block_rows, row_width = latent_cache.shape
    half = blocks_here // 2
    width = w_out.shape[1]
    v_width = w_value.shape[2]
    row_block = steps * heads
    flat_rows = requests * row_block
    me = lax.axis_index("head").astype(jnp.int32)
    smem = pl.BlockSpec(memory_space=pltpu.SMEM)
    vmem = pl.BlockSpec(memory_space=pltpu.VMEM)
    hbm = pl.BlockSpec(memory_space=pltpu.HBM)

    def exchange(x, distance):
        return lax.ppermute(x, "head", [(i, i ^ distance) for i in range(devices)])

    def attend(info, mine, theirs, pieces, first):
        slots = len(pieces) * half
        uses = requests * max_blocks + UNROLL
        return pl.pallas_call(
            functools.partial(
                attend_kernel, len(pieces), first * half, heads, steps, max_blocks, kv_rank,
                float(head_width) ** -0.5,
            ),
            out_shape=(
                jax.ShapeDtypeStruct((flat_rows, kv_rank), jnp.float32),
                jax.ShapeDtypeStruct((flat_rows, LANES), jnp.float32),
                jax.ShapeDtypeStruct((flat_rows, kv_rank + LANES), jnp.bfloat16),
            ),
            in_specs=[smem, vmem, vmem] + [hbm] * len(pieces),
            out_specs=(vmem, vmem, vmem),
            scratch_shapes=[
                pltpu.VMEM((requests, 2 * row_block, row_width), jnp.bfloat16),
                pltpu.VMEM((slots, row_width, block_rows), jnp.bfloat16),
                pltpu.VMEM((min(uses, 2 * slots + UNROLL), 2 * row_block, block_rows), jnp.float32),
                pltpu.VMEM((requests + 1, 2 * row_block, block_rows), jnp.float32),
                pltpu.VMEM((requests + 1, 2 * row_block, block_rows), jnp.float32),
                pltpu.VMEM((requests + 1, 2 * row_block, kv_rank), jnp.float32),
                pltpu.SMEM((uses,), jnp.int32),
                pltpu.SMEM((uses,), jnp.int32),
                pltpu.SMEM((uses,), jnp.int32),
                pltpu.SemaphoreType.DMA((len(pieces),)),
            ],
            compiler_params=pltpu.CompilerParams(vmem_limit_bytes=32 * 1024 * 1024),
            cost_estimate=pl.CostEstimate(
                flops=2 * slots * 2 * row_block * block_rows * 2 * row_width,
                bytes_accessed=slots * block_rows * row_width * 2,
                transcendentals=0,
            ),
            name="attend",
        )(info, mine, theirs, *pieces)

    ring = ring_of(chips)
    up = [
        (ring[i] * 2 + core, ring[(i + 1) % chips] * 2 + core)
        for i in range(chips)
        for core in range(2)
    ]
    down = [(b, a) for a, b in up]
    keys = jnp.swapaxes(latent_cache, 1, 2)
    ups = [keys[:half], keys[half:]]
    downs = list(ups)
    pieces = list(ups)
    partial = []
    done = 0
    for hop in range(1, chips // 2 + 1):
        last = hop == chips // 2
        if hop == 2:
            table = jnp.asarray(slots_by_device(chips, half))
            info = jnp.concatenate(
                [ctx_blocks, owner, block_table.reshape(-1), table[me], me.reshape(1)]
            )
            mine = pl.pallas_call(
                functools.partial(query_kernel, heads),
                out_shape=jax.ShapeDtypeStruct((flat_rows, row_width), jnp.bfloat16),
                in_specs=[vmem, vmem],
                out_specs=vmem,
                scratch_shapes=[
                    pltpu.VMEM((kv_rank // LANES + 1, flat_rows, LANES), jnp.float32)
                ],
                compiler_params=pltpu.CompilerParams(vmem_limit_bytes=16 * 1024 * 1024),
                cost_estimate=pl.CostEstimate(
                    flops=2 * w_absorb.size * row_count, bytes_accessed=2 * w_absorb.size, transcendentals=0
                ),
                name="absorb_queries",
            )(q_heads, w_absorb)
            mine = mine.reshape(requests, row_block, row_width)
            theirs = exchange(mine, 1)
            ups, downs, info, mine = lax.optimization_barrier((ups, downs, info, mine))
        before = list(pieces)
        for part in range(2):
            if not last or part == 0:
                ups[part] = lax.ppermute(ups[part], "head", up)
                pieces.append(ups[part])
            if not last or part == 1:
                downs[part] = lax.ppermute(downs[part], "head", down)
                pieces.append(downs[part])
        if last:
            for stage in (before, pieces[len(before) :]):
                out, lse, away = attend(info, mine, theirs, stage, done)
                partial.append((out, lse, exchange(away, 1)))
                done += len(stage)

    tiles = width // OUT_TILE
    part = jax.ShapeDtypeStruct((chips * steps, width), jnp.bfloat16)
    outs, lses, others = zip(*partial)
    away, keep = pl.pallas_call(
        functools.partial(project_kernel, len(partial), heads, steps, max_blocks, chips),
        out_shape=(part, part),
        in_specs=[smem, vmem, hbm] + [vmem] * (3 * len(partial)),
        out_specs=(vmem, vmem),
        scratch_shapes=[
            pltpu.VMEM((kv_rank // LANES, flat_rows, LANES), jnp.float32),
            pltpu.VMEM((tiles, w_out.shape[0], OUT_TILE), jnp.bfloat16),
            pltpu.VMEM((row_count, heads * v_width), jnp.bfloat16),
            pltpu.SemaphoreType.DMA((tiles,)),
        ],
        compiler_params=pltpu.CompilerParams(vmem_limit_bytes=40 * 1024 * 1024),
        name="merge_and_project",
    )(info, w_value, w_out, *outs, *lses, *others)

    def add(x, *others):
        total = x.astype(jnp.float32)
        for other in others:
            total = total + other.astype(jnp.float32)
        return total.astype(jnp.bfloat16)

    both = add(keep, exchange(away, 1))
    middle = both.shape[0] // 2
    line = add(both[:middle], exchange(both[middle:], 2))
    received = [
        exchange(line[k * steps : (k + 1) * steps], 4 * k) for k in range(1, chips // 2)
    ]
    return add(line[:steps], *received)


def solution(mesh):
    return jax.shard_map(
        local,
        mesh=mesh,
        in_specs=(
            P("group", "head"),
            P("head", None, None),
            P("head", None, None),
            P("head", None),
            P(("group", "head"), None, None),
            P("group"),
            P("group", None),
            P("group"),
        ),
        out_specs=P(("group", "head"), None),
        check_vma=False,
    )
```

```python
import functools
import math

import jax
import jax.numpy as jnp
import numpy as np
from jax import lax
from jax.experimental import pallas as pl
from jax.experimental.pallas import tpu as pltpu
from jax.sharding import PartitionSpec as P

OUT_TILE = 1024
LANES = 128
UNROLL = 4
LATE = 4
EMPTY = -1e30


def ring_of(chips):
    if chips == 8:
        return [0, 2, 4, 6, 7, 5, 3, 1]
    return list(range(chips))


def ring_places(chips):
    places = [(0, 0), (0, 1)]
    for hop in range(1, chips // 2 + 1):
        last = hop == chips // 2
        places += [(-hop, 0), (hop, 1)] if last else [(-hop, 0), (hop, 1), (hop, 0), (-hop, 1)]
    return places


def slots_by_device(chips, half):
    ring = ring_of(chips)
    position = {chip: i for i, chip in enumerate(ring)}
    table = np.full((2 * chips, 4 * chips * half), -1, np.int32)
    for device in range(2 * chips):
        for index, (hop, part) in enumerate(ring_places(chips)):
            source = ring[(position[device // 2] + hop) % chips] * 2 + device % 2
            for i in range(half):
                table[device, (source * 2 + part) * half + i] = index * half + i
    return table


def prepare_kernel(
    heads, steps, cuts,
    me_ref, query_hbm, absorb_hbm, length_hbm, table_hbm, slot_hbm, out_ref, plan_ref,
    query_ref, absorb_ref, length_ref, table_ref, slot_ref, ordered, sems,
):
    sources = (length_hbm, table_hbm, slot_hbm, query_hbm, absorb_hbm)
    targets = (length_ref, table_ref, slot_ref, query_ref, absorb_ref)
    copies = [
        pltpu.make_async_copy(a, b, sems.at[i]) for i, (a, b) in enumerate(zip(sources, targets))
    ]
    for copy in copies:
        copy.start()
    for copy in copies[:3]:
        copy.wait()
    requests = table_ref.shape[0]
    me = me_ref[0]
    stages = len(cuts) - 1
    capacity = plan_ref.shape[0] // stages

    def list_request(r, counts):
        length = length_ref[r]

        def list_block(j, counts):
            slot = slot_ref[me, table_ref[r, j]]
            use = r + 256 * (j == length - 1).astype(jnp.int32)
            counts = list(counts)
            for k in range(stages):
                here = (slot >= cuts[k]) & (slot < cuts[k + 1])
                at = jnp.where(here, counts[k] + 1, capacity - 1)
                plan_ref[k * capacity + at] = use + 512 * (slot - cuts[k])
                counts[k] = counts[k] + here.astype(jnp.int32)
            return tuple(counts)

        return lax.fori_loop(0, length, list_block, counts)

    counts = lax.fori_loop(0, requests, list_request, (jnp.int32(0),) * stages)
    for k in range(stages):
        plan_ref[k * capacity] = counts[k]
        for i in range(UNROLL):
            plan_ref[k * capacity + 1 + counts[k] + i] = requests

    rows = query_ref.shape[0]
    nope = absorb_ref.shape[1]
    head_width = query_ref.shape[1] // heads
    rope = head_width - nope
    kv_rank = absorb_ref.shape[2]
    for copy in copies[3:]:
        copy.wait()
    for h in range(heads):
        own = query_ref[:, h * head_width : (h + 1) * head_width]
        latent = jnp.dot(own[:, :nope], absorb_ref[h], preferred_element_type=jnp.float32)
        turned = jnp.concatenate(
            [own[:, nope:].astype(jnp.float32), jnp.zeros((rows, LANES - rope), jnp.float32)], axis=1
        )
        at = pl.ds(h, rows, stride=heads)
        for c in range(kv_rank // LANES):
            ordered[c, at] = latent[:, c * LANES : (c + 1) * LANES]
        ordered[kv_rank // LANES, at] = turned
    for c in range(kv_rank // LANES):
        out_ref[:, c * LANES : (c + 1) * LANES] = ordered[c].astype(jnp.bfloat16)
    out_ref[:, kv_rank:] = ordered[kv_rank // LANES, :, :rope].astype(jnp.bfloat16)


def attend_kernel(
    piece_count, stage, stages, heads, steps, kv_rank, scale, with_weight,
    plan_ref, mine_ref, theirs_ref, *rest,
):
    pieces, rest = rest[:piece_count], rest[piece_count:]
    if with_weight:
        weight_hbm, out_ref, lse_ref, away_ref, weight_ref, *rest = rest
    else:
        out_ref, lse_ref, away_ref, *rest = rest
    queries, cache, scores, top, total, latent, cache_sems, weight_sems = rest
    requests = top.shape[0] - 1
    row_block = queries.shape[1] // 2
    both = 2 * row_block
    block_rows = cache.shape[2]
    half = cache.shape[0] // piece_count
    base = plan_ref.shape[0] // stages * stage

    copies = [
        pltpu.make_async_copy(p, cache.at[pl.ds(i * half, half)], cache_sems.at[i])
        for i, p in enumerate(pieces)
    ]
    for copy in copies:
        copy.start()
    weight_copies = []
    if with_weight:
        tiles, _, tile = weight_ref.shape
        weight_copies = [
            pltpu.make_async_copy(
                weight_hbm.at[:, pl.ds(i * tile, tile)], weight_ref.at[i], weight_sems.at[i]
            )
            for i in range(tiles)
        ]
        for copy in weight_copies:
            copy.start()

    turns = (plan_ref[base] + UNROLL - 1) // UNROLL
    queries[:, :row_block] = mine_ref[...]
    queries[:, row_block:] = theirs_ref[...]
    top[...] = jnp.full_like(top, -jnp.inf)
    total[...] = jnp.zeros_like(total)
    latent[...] = jnp.zeros_like(latent)
    column = lax.broadcasted_iota(jnp.int32, (both, block_rows), 1)
    row = lax.broadcasted_iota(jnp.int32, (both, block_rows), 0)
    hidden = column + (steps - 1 - (row % row_block) // heads)
    for copy in copies:
        copy.wait()

    def score(turn, _):
        for i in range(UNROLL):
            u = turn * UNROLL + i
            use = plan_ref[base + 1 + u]
            r = use & 255
            s = jnp.dot(
                queries[jnp.minimum(r, requests - 1)], cache[use >> 9],
                preferred_element_type=jnp.float32,
            ) * scale
            seen = (hidden < block_rows) | ((use & 256) == 0)
            s = jnp.where(seen, s, -jnp.inf)
            scores[u] = s
            top[r] = jnp.maximum(top[r], s)
        return 0

    lax.fori_loop(0, turns, score, 0)
    batch = math.gcd(requests, 8)

    def peak(r, _):
        top[r] = jnp.broadcast_to(jnp.max(top[r], axis=1, keepdims=True), (both, block_rows))
        return 0

    lax.fori_loop(0, requests, peak, 0, unroll=batch)

    def mix(turn, _):
        for i in range(UNROLL):
            u = turn * UNROLL + i
            use = plan_ref[base + 1 + u]
            r = use & 255
            p = jnp.exp(scores[u] - top[r])
            total[r] += p
            latent[r] += lax.dot_general(
                p.astype(jnp.bfloat16),
                cache[use >> 9, :kv_rank],
                (((1,), (1,)), ((), ())),
                preferred_element_type=jnp.float32,
            )
        return 0

    lax.fori_loop(0, turns, mix, 0)

    lane = lax.broadcasted_iota(jnp.int32, (row_block, LANES), 1)

    def finish(r, _):
        at = pl.ds(pl.multiple_of(r * row_block, row_block), row_block)
        norm = jnp.sum(total[r], axis=1, keepdims=True)
        some = norm > 0
        safe = jnp.where(some, norm, 1.0)
        lse = jnp.where(some, top[r][:, :1] + jnp.log(safe), EMPTY)
        result = latent[r] * (1.0 / safe)
        out_ref[at] = result[:row_block]
        lse_ref[at] = jnp.broadcast_to(lse[:row_block], (row_block, LANES))
        rest = lse[row_block:]
        high = rest.astype(jnp.bfloat16).astype(jnp.float32)
        middle = (rest - high).astype(jnp.bfloat16).astype(jnp.float32)
        low = rest - high - middle
        terms = jnp.where(lane == 0, high, jnp.where(lane == 1, middle, jnp.where(lane == 2, low, 0.0)))
        away_ref[at, :kv_rank] = result[row_block:].astype(jnp.bfloat16)
        away_ref[at, kv_rank:] = terms.astype(jnp.bfloat16)
        return 0

    lax.fori_loop(0, requests, finish, 0, unroll=batch)
    for copy in weight_copies:
        copy.wait()


def project(placed, weight_ref, first, keep_ref, away_ref):
    tile = weight_ref.shape[2]
    half_rows = keep_ref.shape[0]
    for i in range(keep_ref.shape[1] // tile):
        result = jnp.dot(
            placed, weight_ref[first + i], preferred_element_type=jnp.float32
        ).astype(jnp.bfloat16)
        keep_ref[:, i * tile : (i + 1) * tile] = result[:half_rows]
        away_ref[:, i * tile : (i + 1) * tile] = result[half_rows:]


def merge_kernel(
    stages, heads, steps, chips,
    me_ref, owner_hbm, value_hbm, weight_ref, *rest,
):
    outs, lses, others = rest[:stages], rest[stages : 2 * stages], rest[2 * stages : 3 * stages]
    (away_ref, keep_ref, placed_ref, latent, head_rows, owner_ref, value_ref, sems) = rest[3 * stages :]
    owner_copy = pltpu.make_async_copy(owner_hbm, owner_ref, sems.at[0])
    value_copy = pltpu.make_async_copy(value_hbm, value_ref, sems.at[1])
    owner_copy.start()
    value_copy.start()
    kv_rank, v_width = value_ref.shape[1:]
    rows = head_rows.shape[0]
    requests = rows // steps
    chunk = 64

    def merge(i, _):
        at = pl.ds(pl.multiple_of(i * chunk, chunk), chunk)
        parts = [(o[at], e[at][:, :1]) for o, e in zip(outs, lses)]
        for other in others:
            terms = jnp.sum(other[at, kv_rank:].astype(jnp.float32), axis=1, keepdims=True)
            parts.append((other[at, :kv_rank].astype(jnp.float32), terms))
        peak = functools.reduce(jnp.maximum, [e for _, e in parts])
        shares = [jnp.exp(e - peak) for _, e in parts]
        inverse = 1.0 / functools.reduce(jnp.add, shares)
        whole = functools.reduce(jnp.add, [o * (w * inverse) for (o, _), w in zip(parts, shares)])
        for c in range(kv_rank // LANES):
            latent[c, at] = whole[:, c * LANES : (c + 1) * LANES]
        return 0

    lax.fori_loop(0, rows * heads // chunk, merge, 0, unroll=True)

    value_copy.wait()
    for h in range(heads):
        mine = jnp.concatenate(
            [latent[c, pl.ds(h, rows, stride=heads)] for c in range(kv_rank // LANES)], axis=1
        ).astype(jnp.bfloat16)
        head_rows[:, h * v_width : (h + 1) * v_width] = jnp.dot(
            mine, value_ref[h], preferred_element_type=jnp.float32
        ).astype(jnp.bfloat16)

    half_rows = away_ref.shape[0]
    me = me_ref[0]
    target = lax.broadcasted_iota(jnp.int32, (2 * half_rows, rows), 0)
    origin = lax.broadcasted_iota(jnp.int32, (2 * half_rows, rows), 1)
    owner_copy.wait()

    def place(r, picked):
        apart = owner_ref[r] ^ me
        order = (apart & 1) * chips + ((apart >> 1) & 1) * (chips // 2) + (apart >> 2)
        shifted = origin - r * steps
        hit = (target - order * steps == shifted) & (shifted >= 0) & (shifted < steps)
        return jnp.where(hit, 1.0, picked)

    picker = lax.fori_loop(
        0, requests, place, jnp.zeros((2 * half_rows, rows), jnp.float32), unroll=math.gcd(requests, 8)
    )
    placed = jnp.dot(
        picker.astype(jnp.bfloat16), head_rows[...], preferred_element_type=jnp.float32
    ).astype(jnp.bfloat16)
    placed_ref[...] = placed
    project(placed, weight_ref, 0, keep_ref, away_ref)


def second_kernel(first, placed_ref, weight_ref, away_ref, keep_ref):
    project(placed_ref[...], weight_ref, first, keep_ref, away_ref)


def local(q_heads, w_absorb, w_value, w_out, latent_cache, ctx_blocks, block_table, owner):
    heads, _, kv_rank = w_absorb.shape
    row_count = q_heads.shape[0]
    head_width = q_heads.shape[1] // heads
    requests, max_blocks = block_table.shape
    steps = row_count // requests
    devices = lax.axis_size("head")
    chips = devices // 2
    blocks_here, block_rows, row_width = latent_cache.shape
    half = blocks_here // 2
    width = w_out.shape[1]
    v_width = w_value.shape[2]
    row_block = steps * heads
    flat_rows = requests * row_block
    tiles = width // OUT_TILE
    mebi = 1024 * 1024
    me = lax.axis_index("head").astype(jnp.int32).reshape(1)
    smem = pl.BlockSpec(memory_space=pltpu.SMEM)
    vmem = pl.BlockSpec(memory_space=pltpu.VMEM)
    hbm = pl.BlockSpec(memory_space=pltpu.HBM)

    def exchange(x, distance):
        return lax.ppermute(x, "head", [(i, i ^ distance) for i in range(devices)])

    piece_total = len(ring_places(chips))
    cuts = (0, (piece_total - LATE) * half, piece_total * half)
    stages = len(cuts) - 1
    capacity = requests * max_blocks + UNROLL + 2

    def prepare():
        slots = jnp.asarray(slots_by_device(chips, half))
        queries, plan = pl.pallas_call(
            functools.partial(prepare_kernel, heads, steps, cuts),
            out_shape=(
                jax.ShapeDtypeStruct((flat_rows, row_width), jnp.bfloat16),
                jax.ShapeDtypeStruct((stages * capacity,), jnp.int32),
            ),
            in_specs=[smem] + [hbm] * 5,
            out_specs=(vmem, smem),
            scratch_shapes=[
                pltpu.VMEM(q_heads.shape, jnp.bfloat16),
                pltpu.VMEM(w_absorb.shape, jnp.bfloat16),
                pltpu.SMEM(ctx_blocks.shape, jnp.int32),
                pltpu.SMEM(block_table.shape, jnp.int32),
                pltpu.SMEM(slots.shape, jnp.int32),
                pltpu.VMEM((kv_rank // LANES + 1, flat_rows, LANES), jnp.float32),
                pltpu.SemaphoreType.DMA((5,)),
            ],
            compiler_params=pltpu.CompilerParams(vmem_limit_bytes=8 * mebi),
            cost_estimate=pl.CostEstimate(
                flops=2 * w_absorb.size * row_count, bytes_accessed=4 * w_absorb.size, transcendentals=0
            ),
            name="prepare",
        )(me, q_heads, w_absorb, ctx_blocks, block_table, slots)
        return queries.reshape(requests, row_block, row_width), plan

    def attend(plan, mine, theirs, pieces, stage):
        slots = len(pieces) * half
        with_weight = stage == 0
        weight_shape = jax.ShapeDtypeStruct((tiles, w_out.shape[0], OUT_TILE), jnp.bfloat16)
        return pl.pallas_call(
            functools.partial(
                attend_kernel, len(pieces), stage, stages, heads, steps, kv_rank,
                float(head_width) ** -0.5, with_weight,
            ),
            out_shape=(
                jax.ShapeDtypeStruct((flat_rows, kv_rank), jnp.float32),
                jax.ShapeDtypeStruct((flat_rows, LANES), jnp.float32),
                jax.ShapeDtypeStruct((flat_rows, kv_rank + LANES), jnp.bfloat16),
            ) + (weight_shape,) * with_weight,
            in_specs=[smem, vmem, vmem] + [hbm] * (len(pieces) + with_weight),
            out_specs=(vmem,) * (3 + with_weight),
            scratch_shapes=[
                pltpu.VMEM((requests, 2 * row_block, row_width), jnp.bfloat16),
                pltpu.VMEM((slots, row_width, block_rows), jnp.bfloat16),
                pltpu.VMEM((2 * slots + UNROLL, 2 * row_block, block_rows), jnp.float32),
                pltpu.VMEM((requests + 1, 2 * row_block, block_rows), jnp.float32),
                pltpu.VMEM((requests + 1, 2 * row_block, block_rows), jnp.float32),
                pltpu.VMEM((requests + 1, 2 * row_block, kv_rank), jnp.float32),
                pltpu.SemaphoreType.DMA((len(pieces),)),
                pltpu.SemaphoreType.DMA((tiles,)),
            ],
            compiler_params=pltpu.CompilerParams(vmem_limit_bytes=28 * mebi),
            cost_estimate=pl.CostEstimate(
                flops=2 * slots * 2 * row_block * block_rows * 2 * row_width,
                bytes_accessed=slots * block_rows * row_width * 2,
                transcendentals=0,
            ),
            name="attend",
        )(plan, mine, theirs, *pieces, *([w_out] * with_weight))

    ring = ring_of(chips)
    up = [
        (ring[i] * 2 + core, ring[(i + 1) % chips] * 2 + core)
        for i in range(chips)
        for core in range(2)
    ]
    down = [(b, a) for a, b in up]
    keys = jnp.swapaxes(latent_cache, 1, 2)
    ups = [keys[:half], keys[half:]]
    downs = list(ups)
    pieces = list(ups)
    for hop in range(1, chips // 2 + 1):
        last = hop == chips // 2
        if hop == 2:
            mine, plan = prepare()
            theirs = exchange(mine, 1)
            ups, downs, mine, plan = lax.optimization_barrier((ups, downs, mine, plan))
        if last:
            ups[0] = lax.ppermute(ups[0], "head", up)
            downs[1] = lax.ppermute(downs[1], "head", down)
            pieces += [ups[0], downs[1]]
        else:
            ups[0] = lax.ppermute(ups[0], "head", up)
            downs[1] = lax.ppermute(downs[1], "head", down)
            downs[0] = lax.ppermute(downs[0], "head", down)
            ups[1] = lax.ppermute(ups[1], "head", up)
            pieces += [ups[0], downs[1], downs[0], ups[1]]
    early, late = pieces[:-LATE], pieces[-LATE:]
    *early_part, weight = attend(plan, mine, theirs, early, 0)
    late_part = attend(plan, mine, theirs, late, 1)
    partial = [(out, lse, exchange(away, 1)) for out, lse, away in (early_part, late_part)]

    first = (tiles + 1) // 2
    part_rows = chips * steps
    parts = [
        jax.ShapeDtypeStruct((part_rows, n * OUT_TILE), jnp.bfloat16) for n in (first, tiles - first)
    ]
    placed_shape = jax.ShapeDtypeStruct((2 * part_rows, heads * v_width), jnp.bfloat16)
    outs, lses, others = zip(*partial)
    away, keep, placed = pl.pallas_call(
        functools.partial(merge_kernel, stages, heads, steps, chips),
        out_shape=(parts[0], parts[0], placed_shape),
        in_specs=[smem, hbm, hbm] + [vmem] * (1 + 3 * stages),
        out_specs=(vmem, vmem, vmem),
        scratch_shapes=[
            pltpu.VMEM((kv_rank // LANES, flat_rows, LANES), jnp.float32),
            pltpu.VMEM((row_count, heads * v_width), jnp.bfloat16),
            pltpu.SMEM(owner.shape, jnp.int32),
            pltpu.VMEM(w_value.shape, jnp.bfloat16),
            pltpu.SemaphoreType.DMA((2,)),
        ],
        compiler_params=pltpu.CompilerParams(vmem_limit_bytes=28 * mebi),
        name="merge_and_project",
    )(me, owner, w_value, weight, *outs, *lses, *others)
    away2, keep2 = pl.pallas_call(
        functools.partial(second_kernel, first),
        out_shape=(parts[1], parts[1]),
        in_specs=[vmem, vmem],
        out_specs=(vmem, vmem),
        compiler_params=pltpu.CompilerParams(vmem_limit_bytes=28 * mebi),
        cost_estimate=pl.CostEstimate(
            flops=2 * w_out.size * part_rows, bytes_accessed=w_out.size, transcendentals=0
        ),
        name="project_second",
    )(placed, weight)

    def add(x, *others):
        total = x.astype(jnp.float32)
        for other in others:
            total = total + other.astype(jnp.float32)
        return total.astype(jnp.bfloat16)

    results = []
    for mine_rows, other_rows in ((keep, away), (keep2, away2)):
        both = add(mine_rows, exchange(other_rows, 1))
        middle = part_rows // 2
        line = add(both[:middle], exchange(both[middle:], 2))
        received = [
            exchange(line[k * steps : (k + 1) * steps], 4 * k) for k in range(1, chips // 2)
        ]
        results.append(add(line[:steps], *received))
    return jnp.concatenate(results, axis=1)


def solution(mesh):
    return jax.shard_map(
        local,
        mesh=mesh,
        in_specs=(
            P("group", "head"),
            P("head", None, None),
            P("head", None, None),
            P("head", None),
            P(("group", "head"), None, None),
            P("group"),
            P("group", None),
            P("group"),
        ),
        out_specs=P(("group", "head"), None),
        check_vma=False,
    )
```

```python
import functools
import math

import jax
import jax.numpy as jnp
import numpy as np
from jax import lax
from jax.experimental import pallas as pl
from jax.experimental.pallas import tpu as pltpu
from jax.sharding import PartitionSpec as P

OUT_TILE = 1024
LANES = 128
LATE = 4
TILES = (4, 1, 2)
EMPTY = -1e30


def ring_of(chips):
    if chips == 8:
        return [0, 2, 4, 6, 7, 5, 3, 1]
    return list(range(chips))


def ring_places(chips):
    places = [(0, 0), (0, 1)]
    for hop in range(1, chips // 2 + 1):
        last = hop == chips // 2
        places += [(-hop, 0), (hop, 1)] if last else [(-hop, 0), (hop, 1), (hop, 0), (-hop, 1)]
    return places


def slots_by_device(chips, half):
    ring = ring_of(chips)
    position = {chip: i for i, chip in enumerate(ring)}
    table = np.full((2 * chips, 4 * chips * half), -1, np.int32)
    for device in range(2 * chips):
        for index, (hop, part) in enumerate(ring_places(chips)):
            source = ring[(position[device // 2] + hop) % chips] * 2 + device % 2
            for i in range(half):
                table[device, (source * 2 + part) * half + i] = index * half + i
    return table


def prepare_kernel(
    heads, me_ref, query_hbm, absorb_hbm, length_hbm, table_hbm, slot_hbm, out_ref, plan_ref,
    query_ref, absorb_ref, length_ref, table_ref, slot_ref, ordered, sems,
):
    sources = (length_hbm, table_hbm, slot_hbm, query_hbm, absorb_hbm)
    targets = (length_ref, table_ref, slot_ref, query_ref, absorb_ref)
    copies = [
        pltpu.make_async_copy(a, b, sems.at[i]) for i, (a, b) in enumerate(zip(sources, targets))
    ]
    for copy in copies:
        copy.start()
    requests = table_ref.shape[0]
    entries = plan_ref.shape[0]

    def clear(i, _):
        plan_ref[i] = requests
        return 0

    lax.fori_loop(0, entries, clear, 0)
    for copy in copies[:3]:
        copy.wait()
    me = me_ref[0]

    def list_request(r, _):
        length = length_ref[r]

        def list_block(j, _):
            slot = slot_ref[me, table_ref[r, j]]
            pair = 2 * jnp.where(slot >= 0, slot, entries // 2 - 1)
            at = pair + (plan_ref[pair] != requests).astype(jnp.int32)
            plan_ref[at] = r + 256 * (j == length - 1).astype(jnp.int32)
            return 0

        return lax.fori_loop(0, length, list_block, 0)

    lax.fori_loop(0, requests, list_request, 0)

    rows = query_ref.shape[0]
    nope = absorb_ref.shape[1]
    head_width = query_ref.shape[1] // heads
    rope = head_width - nope
    kv_rank = absorb_ref.shape[2]
    for copy in copies[3:]:
        copy.wait()
    for h in range(heads):
        own = query_ref[:, h * head_width : (h + 1) * head_width]
        latent = jnp.dot(own[:, :nope], absorb_ref[h], preferred_element_type=jnp.float32)
        turned = jnp.concatenate(
            [own[:, nope:].astype(jnp.float32), jnp.zeros((rows, LANES - rope), jnp.float32)], axis=1
        )
        at = pl.ds(h, rows, stride=heads)
        for c in range(kv_rank // LANES):
            ordered[c, at] = latent[:, c * LANES : (c + 1) * LANES]
        ordered[kv_rank // LANES, at] = turned
    for c in range(kv_rank // LANES):
        out_ref[:, c * LANES : (c + 1) * LANES] = ordered[c].astype(jnp.bfloat16)
    out_ref[:, kv_rank:] = ordered[kv_rank // LANES, :, :rope].astype(jnp.bfloat16)


def chip_bits(chips, swap):
    bits = list(range(chips.bit_length() - 1))
    return [bits[1], bits[0]] + bits[2:] if swap else bits


def slot_of(apart, chips, swap):
    order = apart & 1
    for bit in chip_bits(chips, swap):
        order = 2 * order + ((apart >> (bit + 1)) & 1)
    return order


def weight_copy(weight_hbm, first, weight_ref, sems):
    tile = weight_ref.shape[2]
    return [
        pltpu.make_async_copy(
            weight_hbm.at[:, pl.ds((first + i) * tile, tile)], weight_ref.at[i], sems.at[i]
        )
        for i in range(weight_ref.shape[0])
    ]


def attend_kernel(
    piece_count, first_slot, first_tile, heads, steps, kv_rank, scale,
    plan_ref, mine_ref, theirs_ref, *rest,
):
    pieces, rest = rest[:piece_count], rest[piece_count:]
    weight_hbm, out_ref, lse_ref, away_ref, weight_ref, scores, top, total, latent, weight_sems = rest
    row_block = mine_ref.shape[1]
    half = pieces[0].shape[0]
    weight_copies = weight_copy(weight_hbm, first_tile, weight_ref, weight_sems)
    for copy in weight_copies:
        copy.start()

    requests = top.shape[0] - 1
    both = 2 * row_block
    block_rows = pieces[0].shape[2]
    top[...] = jnp.full_like(top, -jnp.inf)
    total[...] = jnp.zeros_like(total)
    latent[...] = jnp.zeros_like(latent)
    column = lax.broadcasted_iota(jnp.int32, (both, block_rows), 1)
    row = lax.broadcasted_iota(jnp.int32, (both, block_rows), 0)
    inside = column + (steps - 1 - (row % row_block) // heads) < block_rows

    def block_of(k):
        return pieces[k // half].at[k % half]

    slots = piece_count * half
    uses = [[plan_ref[2 * (first_slot + k) + i] for i in range(2)] for k in range(slots)]
    users = [[use & 255 for use in pair] for pair in uses]
    for k in range(slots):
        asked = jnp.concatenate(
            [ref[jnp.minimum(r, requests - 1)] for r in users[k] for ref in (mine_ref, theirs_ref)], axis=0
        )
        s = jnp.dot(asked, block_of(k)[...], preferred_element_type=jnp.float32) * scale
        for i in range(2):
            seen = inside | (uses[k][i] < 256)
            part = jnp.where(seen, s[i * both : (i + 1) * both], -jnp.inf)
            scores[k, i * both : (i + 1) * both] = part
            top[users[k][i]] = jnp.maximum(top[users[k][i]], part)

    batch = math.gcd(requests, 8)

    def peak(r, _):
        top[r] = jnp.broadcast_to(jnp.max(top[r], axis=1, keepdims=True), (both, block_rows))
        return 0

    lax.fori_loop(0, requests, peak, 0, unroll=batch)

    for k in range(slots):
        p = jnp.exp(scores[k] - jnp.concatenate([top[r] for r in users[k]], axis=0))
        mixed = lax.dot_general(
            p.astype(jnp.bfloat16),
            block_of(k)[:kv_rank],
            (((1,), (1,)), ((), ())),
            preferred_element_type=jnp.float32,
        )
        for i in range(2):
            total[users[k][i]] += p[i * both : (i + 1) * both]
            latent[users[k][i]] += mixed[i * both : (i + 1) * both]

    lane = lax.broadcasted_iota(jnp.int32, (row_block, LANES), 1)

    def finish(r, _):
        at = pl.ds(pl.multiple_of(r * row_block, row_block), row_block)
        norm = jnp.sum(total[r], axis=1, keepdims=True)
        some = norm > 0
        safe = jnp.where(some, norm, 1.0)
        lse = jnp.where(some, top[r][:, :1] + jnp.log(safe), EMPTY)
        result = latent[r] * (1.0 / safe)
        out_ref[at] = result[:row_block]
        lse_ref[at] = jnp.broadcast_to(lse[:row_block], (row_block, LANES))
        rest = lse[row_block:]
        high = rest.astype(jnp.bfloat16).astype(jnp.float32)
        middle = (rest - high).astype(jnp.bfloat16).astype(jnp.float32)
        low = rest - high - middle
        terms = jnp.where(lane == 0, high, jnp.where(lane == 1, middle, jnp.where(lane == 2, low, 0.0)))
        away_ref[at, :kv_rank] = result[row_block:].astype(jnp.bfloat16)
        away_ref[at, kv_rank:] = terms.astype(jnp.bfloat16)
        return 0

    lax.fori_loop(0, requests, finish, 0, unroll=batch)
    for copy in weight_copies:
        copy.wait()


def project(placed, weights, keep_ref, away_ref):
    half_rows = keep_ref.shape[0]
    at = 0
    for weight_ref in weights:
        tile = weight_ref.shape[2]
        for i in range(weight_ref.shape[0]):
            result = jnp.dot(
                placed, weight_ref[i], preferred_element_type=jnp.float32
            ).astype(jnp.bfloat16)
            keep_ref[:, at : at + tile] = result[:half_rows]
            away_ref[:, at : at + tile] = result[half_rows:]
            at += tile


def merge_kernel(
    stages, first_tile, heads, steps, chips,
    me_ref, owner_hbm, value_hbm, weight_hbm, weight_ref, *rest,
):
    outs, lses, others = rest[:stages], rest[stages : 2 * stages], rest[2 * stages : 3 * stages]
    (away_ref, keep_ref, placed_ref, later_ref,
     latent, head_rows, owner_ref, value_ref, sems, weight_sems) = rest[3 * stages :]
    owner_copy = pltpu.make_async_copy(owner_hbm, owner_ref, sems.at[0])
    value_copy = pltpu.make_async_copy(value_hbm, value_ref, sems.at[1])
    weight_copies = weight_copy(weight_hbm, first_tile, later_ref, weight_sems)
    for copy in (owner_copy, value_copy, *weight_copies):
        copy.start()
    kv_rank, v_width = value_ref.shape[1:]
    rows = head_rows.shape[0]
    requests = rows // steps
    chunk = 64

    def merge(i, _):
        at = pl.ds(pl.multiple_of(i * chunk, chunk), chunk)
        parts = [(o[at], e[at][:, :1]) for o, e in zip(outs, lses)]
        for other in others:
            terms = jnp.sum(other[at, kv_rank:].astype(jnp.float32), axis=1, keepdims=True)
            parts.append((other[at, :kv_rank].astype(jnp.float32), terms))
        peak = functools.reduce(jnp.maximum, [e for _, e in parts])
        shares = [jnp.exp(e - peak) for _, e in parts]
        inverse = 1.0 / functools.reduce(jnp.add, shares)
        whole = functools.reduce(jnp.add, [o * (w * inverse) for (o, _), w in zip(parts, shares)])
        for c in range(kv_rank // LANES):
            latent[c, at] = whole[:, c * LANES : (c + 1) * LANES]
        return 0

    lax.fori_loop(0, rows * heads // chunk, merge, 0, unroll=True)

    half_rows = away_ref.shape[0]
    me = me_ref[0]
    target = lax.broadcasted_iota(jnp.int32, (2 * half_rows, rows), 0)
    origin = lax.broadcasted_iota(jnp.int32, (2 * half_rows, rows), 1)
    owner_copy.wait()

    def place(r, picked):
        apart = owner_ref[r] ^ me
        shifted = origin - r * steps
        row_here = (shifted >= 0) & (shifted < steps)
        return tuple(
            jnp.where((target - slot_of(apart, chips, swap) * steps == shifted) & row_here, 1.0, old)
            for swap, old in enumerate(picked)
        )

    empty = jnp.zeros((2 * half_rows, rows), jnp.float32)
    pickers = lax.fori_loop(0, requests, place, (empty, empty), unroll=math.gcd(requests, 8))

    value_copy.wait()
    for h in range(heads):
        mine = jnp.concatenate(
            [latent[c, pl.ds(h, rows, stride=heads)] for c in range(kv_rank // LANES)], axis=1
        ).astype(jnp.bfloat16)
        head_rows[:, h * v_width : (h + 1) * v_width] = jnp.dot(
            mine, value_ref[h], preferred_element_type=jnp.float32
        ).astype(jnp.bfloat16)

    placed = [
        jnp.dot(
            picker.astype(jnp.bfloat16), head_rows[...], preferred_element_type=jnp.float32
        ).astype(jnp.bfloat16)
        for picker in pickers
    ]
    placed_ref[...] = placed[1]
    project(placed[0], [weight_ref], keep_ref, away_ref)
    for copy in weight_copies:
        copy.wait()


def second_kernel(placed_ref, weight_ref, later_ref, away_ref, keep_ref):
    project(placed_ref[...], [weight_ref, later_ref], keep_ref, away_ref)


def local(q_heads, w_absorb, w_value, w_out, latent_cache, ctx_blocks, block_table, owner):
    heads, _, kv_rank = w_absorb.shape
    row_count = q_heads.shape[0]
    head_width = q_heads.shape[1] // heads
    requests, max_blocks = block_table.shape
    steps = row_count // requests
    devices = lax.axis_size("head")
    chips = devices // 2
    blocks_here, block_rows, row_width = latent_cache.shape
    half = blocks_here // 2
    v_width = w_value.shape[2]
    row_block = steps * heads
    flat_rows = requests * row_block
    mebi = 1024 * 1024
    me = lax.axis_index("head").astype(jnp.int32).reshape(1)
    smem = pl.BlockSpec(memory_space=pltpu.SMEM)
    vmem = pl.BlockSpec(memory_space=pltpu.VMEM)
    hbm = pl.BlockSpec(memory_space=pltpu.HBM)

    def pin(x):
        return pltpu.with_memory_space_constraint(x, pltpu.HBM)

    def exchange(x, distance):
        return lax.ppermute(x, "head", [(i, i ^ distance) for i in range(devices)])

    piece_total = len(ring_places(chips))
    tile_shapes = [
        jax.ShapeDtypeStruct((n, w_out.shape[0], OUT_TILE), jnp.bfloat16) for n in TILES
    ]

    def prepare():
        slots = jnp.asarray(slots_by_device(chips, half))
        queries, plan = pl.pallas_call(
            functools.partial(prepare_kernel, heads),
            out_shape=(
                jax.ShapeDtypeStruct((flat_rows, row_width), jnp.bfloat16),
                jax.ShapeDtypeStruct((2 * piece_total * half + 2,), jnp.int32),
            ),
            in_specs=[smem] + [hbm] * 5,
            out_specs=(vmem, smem),
            scratch_shapes=[
                pltpu.VMEM(q_heads.shape, jnp.bfloat16),
                pltpu.VMEM(w_absorb.shape, jnp.bfloat16),
                pltpu.SMEM(ctx_blocks.shape, jnp.int32),
                pltpu.SMEM(block_table.shape, jnp.int32),
                pltpu.SMEM(slots.shape, jnp.int32),
                pltpu.VMEM((kv_rank // LANES + 1, flat_rows, LANES), jnp.float32),
                pltpu.SemaphoreType.DMA((5,)),
            ],
            compiler_params=pltpu.CompilerParams(vmem_limit_bytes=12 * mebi),
            cost_estimate=pl.CostEstimate(
                flops=2 * w_absorb.size * row_count, bytes_accessed=4 * w_absorb.size, transcendentals=0
            ),
            name="prepare",
        )(me, *map(pin, (q_heads, w_absorb, ctx_blocks, block_table, slots)))
        return queries.reshape(requests, row_block, row_width), plan

    def attend(plan, mine, theirs, pieces, stage):
        slots = len(pieces) * half
        first_slot = 0 if stage == 0 else piece_total * half - slots
        tiles = tile_shapes[stage]
        both = 2 * row_block
        return pl.pallas_call(
            functools.partial(
                attend_kernel, len(pieces), first_slot, sum(TILES[:stage]), heads, steps, kv_rank,
                float(head_width) ** -0.5,
            ),
            out_shape=(
                jax.ShapeDtypeStruct((flat_rows, kv_rank), jnp.float32),
                jax.ShapeDtypeStruct((flat_rows, LANES), jnp.float32),
                jax.ShapeDtypeStruct((flat_rows, kv_rank + LANES), jnp.bfloat16),
                tiles,
            ),
            in_specs=[smem] + [vmem] * (2 + len(pieces)) + [hbm],
            out_specs=(vmem,) * 4,
            scratch_shapes=[
                pltpu.VMEM((slots, 2 * both, block_rows), jnp.float32),
                pltpu.VMEM((requests + 1, both, block_rows), jnp.float32),
                pltpu.VMEM((requests + 1, both, block_rows), jnp.float32),
                pltpu.VMEM((requests + 1, both, kv_rank), jnp.float32),
                pltpu.SemaphoreType.DMA((tiles.shape[0],)),
            ],
            compiler_params=pltpu.CompilerParams(vmem_limit_bytes=28 * mebi),
            cost_estimate=pl.CostEstimate(
                flops=2 * slots * 2 * both * block_rows * 2 * row_width,
                bytes_accessed=slots * block_rows * row_width * 2,
                transcendentals=0,
            ),
            name="attend",
        )(plan, mine, theirs, *pieces, pin(w_out))

    ring = ring_of(chips)
    up = [
        (ring[i] * 2 + core, ring[(i + 1) % chips] * 2 + core)
        for i in range(chips)
        for core in range(2)
    ]
    down = [(b, a) for a, b in up]
    keys = jnp.swapaxes(latent_cache, 1, 2)
    ups = [keys[:half], keys[half:]]
    downs = list(ups)
    pieces = list(ups)
    for hop in range(1, chips // 2 + 1):
        last = hop == chips // 2
        if hop == 2:
            mine, plan = prepare()
            theirs = exchange(mine, 1)
            ups[0], mine, plan = lax.optimization_barrier((ups[0], mine, plan))
        if last:
            ups[0] = lax.ppermute(ups[0], "head", up)
            downs[1] = lax.ppermute(downs[1], "head", down)
            pieces += [ups[0], downs[1]]
        else:
            ups[0] = lax.ppermute(ups[0], "head", up)
            downs[1] = lax.ppermute(downs[1], "head", down)
            downs[0] = lax.ppermute(downs[0], "head", down)
            ups[1] = lax.ppermute(ups[1], "head", up)
            pieces += [ups[0], downs[1], downs[0], ups[1]]
    early, late = pieces[:-LATE], pieces[-LATE:]
    *early_part, weight = attend(plan, mine, theirs, early, 0)
    *late_part, next_weight = attend(plan, mine, theirs, late, 1)
    partial = [(out, lse, exchange(away, 1)) for out, lse, away in (early_part, late_part)]

    part_rows = chips * steps
    widths = (TILES[0] * OUT_TILE, (TILES[1] + TILES[2]) * OUT_TILE)
    parts = [jax.ShapeDtypeStruct((part_rows, n), jnp.bfloat16) for n in widths]
    placed_shape = jax.ShapeDtypeStruct((2 * part_rows, heads * v_width), jnp.bfloat16)
    outs, lses, others = zip(*partial)
    away, keep, placed, last_weight = pl.pallas_call(
        functools.partial(
            merge_kernel, len(partial), TILES[0] + TILES[1], heads, steps, chips
        ),
        out_shape=(parts[0], parts[0], placed_shape, tile_shapes[2]),
        in_specs=[smem, hbm, hbm, hbm] + [vmem] * (1 + 3 * len(partial)),
        out_specs=(vmem,) * 4,
        scratch_shapes=[
            pltpu.VMEM((kv_rank // LANES, flat_rows, LANES), jnp.float32),
            pltpu.VMEM((row_count, heads * v_width), jnp.bfloat16),
            pltpu.SMEM(owner.shape, jnp.int32),
            pltpu.VMEM(w_value.shape, jnp.bfloat16),
            pltpu.SemaphoreType.DMA((2,)),
            pltpu.SemaphoreType.DMA((TILES[2],)),
        ],
        compiler_params=pltpu.CompilerParams(vmem_limit_bytes=28 * mebi),
        name="merge_and_project",
    )(me, pin(owner), pin(w_value), pin(w_out), weight, *outs, *lses, *others)
    next_away, next_keep = pl.pallas_call(
        second_kernel,
        out_shape=(parts[1], parts[1]),
        in_specs=[vmem] * 3,
        out_specs=(vmem, vmem),
        compiler_params=pltpu.CompilerParams(vmem_limit_bytes=28 * mebi),
        cost_estimate=pl.CostEstimate(
            flops=2 * w_out.size * part_rows, bytes_accessed=8 * w_out.size, transcendentals=0
        ),
        name="project_second",
    )(placed, next_weight, last_weight)

    def add(x, y):
        return (x.astype(jnp.float32) + y.astype(jnp.float32)).astype(jnp.bfloat16)

    def fold(x, bit):
        middle = x.shape[0] // 2
        return add(x[:middle], exchange(x[middle:], 2 << bit))

    halves = [add(keep, exchange(away, 1)), add(next_keep, exchange(next_away, 1))]
    for step in range(2):
        halves = [fold(x, chip_bits(chips, swap)[step]) for swap, x in enumerate(halves)]
    result = jnp.concatenate(halves, axis=1)
    for bit in chip_bits(chips, False)[2:]:
        result = fold(result, bit)
    return result


def solution(mesh):
    return jax.shard_map(
        local,
        mesh=mesh,
        in_specs=(
            P("group", "head"),
            P("head", None, None),
            P("head", None, None),
            P("head", None),
            P(("group", "head"), None, None),
            P("group"),
            P("group", None),
            P("group"),
        ),
        out_specs=P(("group", "head"), None),
        check_vma=False,
    )
```

```python
import functools
import math

import jax
import jax.numpy as jnp
import numpy as np
from jax import lax
from jax.experimental import pallas as pl
from jax.experimental.pallas import tpu as pltpu
from jax.sharding import PartitionSpec as P

OUT_TILE = 1024
LANES = 128
LATE = 4
TILES = (3, 4)
FIRST = 3
EMPTY = -1e30


def ring_of(chips):
    if chips == 8:
        return [0, 2, 4, 6, 7, 5, 3, 1]
    return list(range(chips))


def ring_places(chips):
    places = [(0, 0), (0, 1)]
    for hop in range(1, chips // 2 + 1):
        last = hop == chips // 2
        places += [(-hop, 0), (hop, 1)] if last else [(-hop, 0), (hop, 1), (hop, 0), (-hop, 1)]
    return places


def slots_by_device(chips, half):
    ring = ring_of(chips)
    position = {chip: i for i, chip in enumerate(ring)}
    table = np.full((2 * chips, 4 * chips * half), -1, np.int32)
    for device in range(2 * chips):
        for index, (hop, part) in enumerate(ring_places(chips)):
            source = ring[(position[device // 2] + hop) % chips] * 2 + device % 2
            for i in range(half):
                table[device, (source * 2 + part) * half + i] = index * half + i
    return table


def prepare_kernel(
    heads, chips, me_ref, query_hbm, absorb_hbm, length_hbm, table_hbm, slot_hbm, owner_hbm, weight_hbm,
    out_ref, plan_ref, order_ref, weight_ref,
    query_ref, absorb_ref, length_ref, table_ref, slot_ref, owner_ref, ordered, sems, weight_sems,
):
    sources = (length_hbm, table_hbm, slot_hbm, owner_hbm, query_hbm, absorb_hbm)
    targets = (length_ref, table_ref, slot_ref, owner_ref, query_ref, absorb_ref)
    copies = [
        pltpu.make_async_copy(a, b, sems.at[i]) for i, (a, b) in enumerate(zip(sources, targets))
    ]
    weight_copies = weight_copy(weight_hbm, 0, weight_ref, weight_sems)
    for copy in copies + weight_copies:
        copy.start()
    requests = table_ref.shape[0]
    entries = plan_ref.shape[0]

    def clear(i, _):
        plan_ref[i] = requests
        return 0

    lax.fori_loop(0, entries, clear, 0)
    for copy in copies[:4]:
        copy.wait()
    me = me_ref[0]

    def list_request(r, _):
        length = length_ref[r]
        order_ref[r] = slot_of(owner_ref[r] ^ me, chips)

        def list_block(j, _):
            slot = slot_ref[me, table_ref[r, j]]
            pair = 2 * jnp.where(slot >= 0, slot, entries // 2 - 1)
            at = pair + (plan_ref[pair] != requests).astype(jnp.int32)
            plan_ref[at] = r + 256 * (j == length - 1).astype(jnp.int32)
            return 0

        return lax.fori_loop(0, length, list_block, 0)

    lax.fori_loop(0, requests, list_request, 0)

    rows = query_ref.shape[0]
    nope = absorb_ref.shape[1]
    head_width = query_ref.shape[1] // heads
    rope = head_width - nope
    kv_rank = absorb_ref.shape[2]
    for copy in copies[4:]:
        copy.wait()
    for h in range(heads):
        own = query_ref[:, h * head_width : (h + 1) * head_width]
        latent = jnp.dot(own[:, :nope], absorb_ref[h], preferred_element_type=jnp.float32)
        turned = jnp.concatenate(
            [own[:, nope:].astype(jnp.float32), jnp.zeros((rows, LANES - rope), jnp.float32)], axis=1
        )
        at = pl.ds(h, rows, stride=heads)
        for c in range(kv_rank // LANES):
            ordered[c, at] = latent[:, c * LANES : (c + 1) * LANES]
        ordered[kv_rank // LANES, at] = turned
    for c in range(kv_rank // LANES):
        out_ref[:, c * LANES : (c + 1) * LANES] = ordered[c].astype(jnp.bfloat16)
    out_ref[:, kv_rank:] = ordered[kv_rank // LANES, :, :rope].astype(jnp.bfloat16)
    for copy in weight_copies:
        copy.wait()


def slot_of(apart, chips):
    return (apart & 1) * chips + ((apart >> 1) & 1) * (chips // 2) + (apart >> 2)


def weight_copy(weight_hbm, first, weight_ref, sems):
    tile = weight_ref.shape[2]
    return [
        pltpu.make_async_copy(
            weight_hbm.at[:, pl.ds((first + i) * tile, tile)], weight_ref.at[i], sems.at[i]
        )
        for i in range(weight_ref.shape[0])
    ]


def attend_kernel(
    piece_count, first_slot, first_tile, heads, steps, kv_rank, scale,
    plan_ref, mine_ref, theirs_ref, *rest,
):
    pieces, rest = rest[:piece_count], rest[piece_count:]
    weight_copies = []
    if first_tile:
        weight_hbm, out_ref, lse_ref, away_ref, weight_ref, *rest, weight_sems = rest
        weight_copies = weight_copy(weight_hbm, first_tile, weight_ref, weight_sems)
    else:
        out_ref, lse_ref, away_ref, *rest = rest
    scores, top, total, latent = rest
    row_block = mine_ref.shape[1]
    half = pieces[0].shape[0]
    for copy in weight_copies:
        copy.start()

    requests = top.shape[0] - 1
    both = 2 * row_block
    block_rows = pieces[0].shape[2]
    top[...] = jnp.full_like(top, -jnp.inf)
    total[...] = jnp.zeros_like(total)
    latent[...] = jnp.zeros_like(latent)
    column = lax.broadcasted_iota(jnp.int32, (both, block_rows), 1)
    row = lax.broadcasted_iota(jnp.int32, (both, block_rows), 0)
    inside = column + (steps - 1 - (row % row_block) // heads) < block_rows

    def block_of(k):
        return pieces[k // half].at[k % half]

    slots = piece_count * half
    uses = [[plan_ref[2 * (first_slot + k) + i] for i in range(2)] for k in range(slots)]
    users = [[use & 255 for use in pair] for pair in uses]
    for k in range(slots):
        asked = jnp.concatenate(
            [ref[jnp.minimum(r, requests - 1)] for r in users[k] for ref in (mine_ref, theirs_ref)], axis=0
        )
        s = jnp.dot(asked, block_of(k)[...], preferred_element_type=jnp.float32) * scale
        for i in range(2):
            seen = inside | (uses[k][i] < 256)
            part = jnp.where(seen, s[i * both : (i + 1) * both], -jnp.inf)
            scores[k, i * both : (i + 1) * both] = part
            top[users[k][i]] = jnp.maximum(top[users[k][i]], part)

    batch = math.gcd(requests, 8)

    def peak(r, _):
        top[r] = jnp.broadcast_to(jnp.max(top[r], axis=1, keepdims=True), (both, block_rows))
        return 0

    lax.fori_loop(0, requests, peak, 0, unroll=batch)

    for k in range(slots):
        p = jnp.exp(scores[k] - jnp.concatenate([top[r] for r in users[k]], axis=0))
        mixed = lax.dot_general(
            p.astype(jnp.bfloat16),
            block_of(k)[:kv_rank],
            (((1,), (1,)), ((), ())),
            preferred_element_type=jnp.float32,
        )
        for i in range(2):
            total[users[k][i]] += p[i * both : (i + 1) * both]
            latent[users[k][i]] += mixed[i * both : (i + 1) * both]

    lane = lax.broadcasted_iota(jnp.int32, (row_block, LANES), 1)

    def finish(r, _):
        at = pl.ds(pl.multiple_of(r * row_block, row_block), row_block)
        norm = jnp.sum(total[r], axis=1, keepdims=True)
        some = norm > 0
        safe = jnp.where(some, norm, 1.0)
        lse = jnp.where(some, top[r][:, :1] + jnp.log(safe), EMPTY)
        result = latent[r] * (1.0 / safe)
        out_ref[at] = result[:row_block]
        lse_ref[at] = jnp.broadcast_to(lse[:row_block], (row_block, LANES))
        rest = lse[row_block:]
        high = rest.astype(jnp.bfloat16).astype(jnp.float32)
        middle = (rest - high).astype(jnp.bfloat16).astype(jnp.float32)
        low = rest - high - middle
        terms = jnp.where(lane == 0, high, jnp.where(lane == 1, middle, jnp.where(lane == 2, low, 0.0)))
        away_ref[at, :kv_rank] = result[row_block:].astype(jnp.bfloat16)
        away_ref[at, kv_rank:] = terms.astype(jnp.bfloat16)
        return 0

    lax.fori_loop(0, requests, finish, 0, unroll=batch)
    for copy in weight_copies:
        copy.wait()


def tiles_of(*weights):
    return [(ref, i) for ref in weights for i in range(ref.shape[0])]


def project(placed, tiles, keep_ref, away_ref):
    half_rows = keep_ref.shape[0]
    at = 0
    for weight_ref, i in tiles:
        tile = weight_ref.shape[2]
        result = jnp.dot(
            placed, weight_ref[i], preferred_element_type=jnp.float32
        ).astype(jnp.bfloat16)
        keep_ref[:, at : at + tile] = result[:half_rows]
        away_ref[:, at : at + tile] = result[half_rows:]
        at += tile


def merge_kernel(
    stages, heads, steps, order_ref, value_ref, weight_ref, next_ref, *rest,
):
    outs, lses, others = rest[:stages], rest[stages : 2 * stages], rest[2 * stages : 3 * stages]
    away_ref, keep_ref, placed_ref, latent, head_rows = rest[3 * stages :]
    kv_rank, v_width = value_ref.shape[1:]
    rows = head_rows.shape[0]
    requests = rows // steps
    chunk = 64

    def merge(i, _):
        at = pl.ds(pl.multiple_of(i * chunk, chunk), chunk)
        parts = [(o[at], e[at][:, :1]) for o, e in zip(outs, lses)]
        for other in others:
            terms = jnp.sum(other[at, kv_rank:].astype(jnp.float32), axis=1, keepdims=True)
            parts.append((other[at, :kv_rank].astype(jnp.float32), terms))
        peak = functools.reduce(jnp.maximum, [e for _, e in parts])
        shares = [jnp.exp(e - peak) for _, e in parts]
        inverse = 1.0 / functools.reduce(jnp.add, shares)
        whole = functools.reduce(jnp.add, [o * (w * inverse) for (o, _), w in zip(parts, shares)])
        for c in range(kv_rank // LANES):
            latent[c, at] = whole[:, c * LANES : (c + 1) * LANES]
        return 0

    lax.fori_loop(0, rows * heads // chunk, merge, 0, unroll=True)

    half_rows = away_ref.shape[0]
    target = lax.broadcasted_iota(jnp.int32, (2 * half_rows, rows), 0)
    origin = lax.broadcasted_iota(jnp.int32, (2 * half_rows, rows), 1)

    def place(r, picked):
        shifted = origin - r * steps
        hit = (target - order_ref[r] * steps == shifted) & (shifted >= 0) & (shifted < steps)
        return jnp.where(hit, 1.0, picked)

    picker = lax.fori_loop(
        0, requests, place, jnp.zeros((2 * half_rows, rows), jnp.float32), unroll=math.gcd(requests, 8)
    )

    for h in range(heads):
        mine = jnp.concatenate(
            [latent[c, pl.ds(h, rows, stride=heads)] for c in range(kv_rank // LANES)], axis=1
        ).astype(jnp.bfloat16)
        head_rows[:, h * v_width : (h + 1) * v_width] = jnp.dot(
            mine, value_ref[h], preferred_element_type=jnp.float32
        ).astype(jnp.bfloat16)

    placed = jnp.dot(
        picker.astype(jnp.bfloat16), head_rows[...], preferred_element_type=jnp.float32
    ).astype(jnp.bfloat16)
    placed_ref[...] = placed
    project(placed, tiles_of(weight_ref, next_ref)[:FIRST], keep_ref, away_ref)


def second_kernel(placed_ref, weight_ref, next_ref, away_ref, keep_ref):
    tiles = tiles_of(weight_ref, next_ref)
    project(placed_ref[...], tiles[FIRST:], keep_ref, away_ref)


def local(q_heads, w_absorb, w_value, w_out, latent_cache, ctx_blocks, block_table, owner):
    heads, _, kv_rank = w_absorb.shape
    row_count = q_heads.shape[0]
    head_width = q_heads.shape[1] // heads
    requests, max_blocks = block_table.shape
    steps = row_count // requests
    devices = lax.axis_size("head")
    chips = devices // 2
    blocks_here, block_rows, row_width = latent_cache.shape
    half = blocks_here // 2
    v_width = w_value.shape[2]
    row_block = steps * heads
    flat_rows = requests * row_block
    mebi = 1024 * 1024
    me = lax.axis_index("head").astype(jnp.int32).reshape(1)
    smem = pl.BlockSpec(memory_space=pltpu.SMEM)
    vmem = pl.BlockSpec(memory_space=pltpu.VMEM)
    hbm = pl.BlockSpec(memory_space=pltpu.HBM)

    def pin(x):
        return pltpu.with_memory_space_constraint(x, pltpu.HBM)

    def add(x, *others):
        total = x.astype(jnp.float32)
        for other in others:
            total = total + other.astype(jnp.float32)
        return total.astype(jnp.bfloat16)

    def fold(x, distance):
        middle = x.shape[0] // 2
        return add(x[:middle], exchange(x[middle:], distance))

    def exchange(x, distance):
        return lax.ppermute(x, "head", [(i, i ^ distance) for i in range(devices)])

    piece_total = len(ring_places(chips))
    tile_shapes = [
        jax.ShapeDtypeStruct((n, w_out.shape[0], OUT_TILE), jnp.bfloat16) for n in TILES
    ]

    def prepare():
        slots = jnp.asarray(slots_by_device(chips, half))
        queries, plan, order, weight = pl.pallas_call(
            functools.partial(prepare_kernel, heads, chips),
            out_shape=(
                jax.ShapeDtypeStruct((flat_rows, row_width), jnp.bfloat16),
                jax.ShapeDtypeStruct((2 * piece_total * half + 2,), jnp.int32),
                jax.ShapeDtypeStruct((requests,), jnp.int32),
                tile_shapes[0],
            ),
            in_specs=[smem] + [hbm] * 7,
            out_specs=(vmem, smem, smem, vmem),
            scratch_shapes=[
                pltpu.VMEM(q_heads.shape, jnp.bfloat16),
                pltpu.VMEM(w_absorb.shape, jnp.bfloat16),
                pltpu.SMEM(ctx_blocks.shape, jnp.int32),
                pltpu.SMEM(block_table.shape, jnp.int32),
                pltpu.SMEM(slots.shape, jnp.int32),
                pltpu.SMEM(owner.shape, jnp.int32),
                pltpu.VMEM((kv_rank // LANES + 1, flat_rows, LANES), jnp.float32),
                pltpu.SemaphoreType.DMA((6,)),
                pltpu.SemaphoreType.DMA((TILES[0],)),
            ],
            compiler_params=pltpu.CompilerParams(vmem_limit_bytes=12 * mebi),
            cost_estimate=pl.CostEstimate(
                flops=2 * w_absorb.size * row_count, bytes_accessed=4 * w_absorb.size, transcendentals=0
            ),
            name="prepare",
        )(me, *map(pin, (q_heads, w_absorb, ctx_blocks, block_table, slots, owner, w_out)))
        return queries.reshape(requests, row_block, row_width), plan, order, weight

    def attend(plan, mine, theirs, pieces, stage):
        slots = len(pieces) * half
        first_slot = 0 if stage == 0 else piece_total * half - slots
        with_weight = stage == 0
        both = 2 * row_block
        return pl.pallas_call(
            functools.partial(
                attend_kernel, len(pieces), first_slot, TILES[0] * with_weight, heads, steps, kv_rank,
                float(head_width) ** -0.5,
            ),
            out_shape=(
                jax.ShapeDtypeStruct((flat_rows, kv_rank), jnp.float32),
                jax.ShapeDtypeStruct((flat_rows, LANES), jnp.float32),
                jax.ShapeDtypeStruct((flat_rows, kv_rank + LANES), jnp.bfloat16),
            ) + (tile_shapes[1],) * with_weight,
            in_specs=[smem] + [vmem] * (2 + len(pieces)) + [hbm] * with_weight,
            out_specs=(vmem,) * (3 + with_weight),
            scratch_shapes=[
                pltpu.VMEM((slots, 2 * both, block_rows), jnp.float32),
                pltpu.VMEM((requests + 1, both, block_rows), jnp.float32),
                pltpu.VMEM((requests + 1, both, block_rows), jnp.float32),
                pltpu.VMEM((requests + 1, both, kv_rank), jnp.float32),
            ] + [pltpu.SemaphoreType.DMA((TILES[1],))] * with_weight,
            compiler_params=pltpu.CompilerParams(vmem_limit_bytes=28 * mebi),
            cost_estimate=pl.CostEstimate(
                flops=2 * slots * 2 * both * block_rows * 2 * row_width,
                bytes_accessed=slots * block_rows * row_width * 2,
                transcendentals=0,
            ),
            name="attend",
        )(plan, mine, theirs, *pieces, *([pin(w_out)] * with_weight))

    ring = ring_of(chips)
    up = [
        (ring[i] * 2 + core, ring[(i + 1) % chips] * 2 + core)
        for i in range(chips)
        for core in range(2)
    ]
    down = [(b, a) for a, b in up]
    keys = jnp.swapaxes(latent_cache, 1, 2)
    ups = [keys[:half], keys[half:]]
    downs = list(ups)
    pieces = list(ups)
    for hop in range(1, chips // 2 + 1):
        last = hop == chips // 2
        if hop == 2:
            mine, plan, order, weight = prepare()
            theirs = exchange(mine, 1)
            ups[0], mine, plan = lax.optimization_barrier((ups[0], mine, plan))
        if last:
            ups[0] = lax.ppermute(ups[0], "head", up)
            downs[1] = lax.ppermute(downs[1], "head", down)
            pieces += [ups[0], downs[1]]
        else:
            ups[0] = lax.ppermute(ups[0], "head", up)
            downs[1] = lax.ppermute(downs[1], "head", down)
            downs[0] = lax.ppermute(downs[0], "head", down)
            ups[1] = lax.ppermute(ups[1], "head", up)
            pieces += [ups[0], downs[1], downs[0], ups[1]]
    early, late = pieces[:-LATE], pieces[-LATE:]
    *early_part, next_weight = attend(plan, mine, theirs, early, 0)
    late_part = attend(plan, mine, theirs, late, 1)
    partial = [(out, lse, exchange(away, 1)) for out, lse, away in (early_part, late_part)]

    part_rows = chips * steps
    widths = (FIRST * OUT_TILE, (sum(TILES) - FIRST) * OUT_TILE)
    parts = [jax.ShapeDtypeStruct((part_rows, n), jnp.bfloat16) for n in widths]
    placed_shape = jax.ShapeDtypeStruct((2 * part_rows, heads * v_width), jnp.bfloat16)
    outs, lses, others = zip(*partial)
    away, keep, placed = pl.pallas_call(
        functools.partial(merge_kernel, len(partial), heads, steps),
        out_shape=(parts[0], parts[0], placed_shape),
        in_specs=[smem] + [vmem] * (3 + 3 * len(partial)),
        out_specs=(vmem,) * 3,
        scratch_shapes=[
            pltpu.VMEM((kv_rank // LANES, flat_rows, LANES), jnp.float32),
            pltpu.VMEM((row_count, heads * v_width), jnp.bfloat16),
        ],
        compiler_params=pltpu.CompilerParams(vmem_limit_bytes=28 * mebi),
        name="merge_and_project",
    )(order, w_value, weight, next_weight, *outs, *lses, *others)
    first_half = add(keep, exchange(away, 1))
    next_away, next_keep = pl.pallas_call(
        second_kernel,
        out_shape=(parts[1], parts[1]),
        in_specs=[vmem] * 3,
        out_specs=(vmem, vmem),
        compiler_params=pltpu.CompilerParams(vmem_limit_bytes=28 * mebi),
        cost_estimate=pl.CostEstimate(
            flops=2 * w_out.size * part_rows, bytes_accessed=8 * w_out.size, transcendentals=0
        ),
        name="project_second",
    )(placed, weight, next_weight)

    second_half = add(next_keep, exchange(next_away, 1))
    result = jnp.concatenate([fold(first_half, 2), fold(second_half, 2)], axis=1)
    distance = 4
    while result.shape[0] > 4 * steps:
        result = fold(result, distance)
        distance *= 2
    ways = result.shape[0] // steps
    received = [
        exchange(result[k * steps : (k + 1) * steps], distance * k) for k in range(1, ways)
    ]
    return add(result[:steps], *received)


def solution(mesh):
    return jax.shard_map(
        local,
        mesh=mesh,
        in_specs=(
            P("group", "head"),
            P("head", None, None),
            P("head", None, None),
            P("head", None),
            P(("group", "head"), None, None),
            P("group"),
            P("group", None),
            P("group"),
        ),
        out_specs=P(("group", "head"), None),
        check_vma=False,
    )
```

```python
import functools
import math

import jax
import jax.numpy as jnp
import numpy as np
from jax import lax
from jax.experimental import pallas as pl
from jax.experimental.pallas import tpu as pltpu
from jax.sharding import PartitionSpec as P

OUT_TILE = 1024
LANES = 128
LATE = 4
FIRST = 3
COVER = 30_000_000_000
EMPTY = -1e30


def ring_of(chips):
    if chips == 8:
        return [0, 2, 4, 6, 7, 5, 3, 1]
    return list(range(chips))


def ring_places(chips):
    places = [(0, 0), (0, 1)]
    for hop in range(1, chips // 2 + 1):
        last = hop == chips // 2
        places += [(-hop, 0), (hop, 1)] if last else [(-hop, 0), (hop, 1), (hop, 0), (-hop, 1)]
    return places


def slots_by_device(chips, half):
    ring = ring_of(chips)
    position = {chip: i for i, chip in enumerate(ring)}
    table = np.full((2 * chips, 4 * chips * half), -1, np.int32)
    for device in range(2 * chips):
        for index, (hop, part) in enumerate(ring_places(chips)):
            source = ring[(position[device // 2] + hop) % chips] * 2 + device % 2
            for i in range(half):
                table[device, (source * 2 + part) * half + i] = index * half + i
    return table


def prepare_kernel(
    heads, chips, me_ref, query_hbm, absorb_hbm, length_hbm, table_hbm, slot_hbm, owner_hbm,
    out_ref, plan_ref, order_ref,
    query_ref, absorb_ref, length_ref, table_ref, slot_ref, owner_ref, ordered, sems,
):
    sources = (length_hbm, table_hbm, slot_hbm, owner_hbm, query_hbm, absorb_hbm)
    targets = (length_ref, table_ref, slot_ref, owner_ref, query_ref, absorb_ref)
    copies = [
        pltpu.make_async_copy(a, b, sems.at[i]) for i, (a, b) in enumerate(zip(sources, targets))
    ]
    for copy in copies:
        copy.start()
    requests = table_ref.shape[0]
    entries = plan_ref.shape[0]

    def clear(i, _):
        plan_ref[i] = requests
        return 0

    lax.fori_loop(0, entries, clear, 0)
    for copy in copies[:4]:
        copy.wait()
    me = me_ref[0]

    def list_request(r, _):
        length = length_ref[r]
        order_ref[r] = slot_of(owner_ref[r] ^ me, chips)

        def list_block(j, _):
            slot = slot_ref[me, table_ref[r, j]]
            pair = 2 * jnp.where(slot >= 0, slot, entries // 2 - 1)
            at = pair + (plan_ref[pair] != requests).astype(jnp.int32)
            plan_ref[at] = r + 256 * (j == length - 1).astype(jnp.int32)
            return 0

        return lax.fori_loop(0, length, list_block, 0)

    lax.fori_loop(0, requests, list_request, 0)

    rows = query_ref.shape[0]
    nope = absorb_ref.shape[1]
    head_width = query_ref.shape[1] // heads
    rope = head_width - nope
    kv_rank = absorb_ref.shape[2]
    for copy in copies[4:]:
        copy.wait()
    for h in range(heads):
        own = query_ref[:, h * head_width : (h + 1) * head_width]
        latent = jnp.dot(own[:, :nope], absorb_ref[h], preferred_element_type=jnp.float32)
        turned = jnp.concatenate(
            [own[:, nope:].astype(jnp.float32), jnp.zeros((rows, LANES - rope), jnp.float32)], axis=1
        )
        at = pl.ds(h, rows, stride=heads)
        for c in range(kv_rank // LANES):
            ordered[c, at] = latent[:, c * LANES : (c + 1) * LANES]
        ordered[kv_rank // LANES, at] = turned
    for c in range(kv_rank // LANES):
        out_ref[:, c * LANES : (c + 1) * LANES] = ordered[c].astype(jnp.bfloat16)
    out_ref[:, kv_rank:] = ordered[kv_rank // LANES, :, :rope].astype(jnp.bfloat16)


def slot_of(apart, chips):
    return (apart & 1) * chips + ((apart >> 1) & 1) * (chips // 2) + (apart >> 2)


def attend_kernel(
    piece_count, first_slot, heads, steps, kv_rank, scale,
    plan_ref, mine_ref, theirs_ref, *rest,
):
    pieces, rest = rest[:piece_count], rest[piece_count:]
    out_ref, lse_ref, away_ref, scores, top, total, latent = rest
    row_block = mine_ref.shape[1]
    half = pieces[0].shape[0]
    requests = top.shape[0] - 1
    both = 2 * row_block
    block_rows = pieces[0].shape[2]
    top[...] = jnp.full_like(top, -jnp.inf)
    total[...] = jnp.zeros_like(total)
    latent[...] = jnp.zeros_like(latent)
    column = lax.broadcasted_iota(jnp.int32, (both, block_rows), 1)
    row = lax.broadcasted_iota(jnp.int32, (both, block_rows), 0)
    inside = column + (steps - 1 - (row % row_block) // heads) < block_rows

    def block_of(k):
        return pieces[k // half].at[k % half]

    slots = piece_count * half
    uses = [[plan_ref[2 * (first_slot + k) + i] for i in range(2)] for k in range(slots)]
    users = [[use & 255 for use in pair] for pair in uses]
    for k in range(slots):
        asked = jnp.concatenate(
            [ref[jnp.minimum(r, requests - 1)] for r in users[k] for ref in (mine_ref, theirs_ref)], axis=0
        )
        s = jnp.dot(asked, block_of(k)[...], preferred_element_type=jnp.float32) * scale
        for i in range(2):
            seen = inside | (uses[k][i] < 256)
            part = jnp.where(seen, s[i * both : (i + 1) * both], -jnp.inf)
            scores[k, i * both : (i + 1) * both] = part
            top[users[k][i]] = jnp.maximum(top[users[k][i]], part)

    batch = math.gcd(requests, 8)

    def peak(r, _):
        top[r] = jnp.broadcast_to(jnp.max(top[r], axis=1, keepdims=True), (both, block_rows))
        return 0

    lax.fori_loop(0, requests, peak, 0, unroll=batch)

    for k in range(slots):
        p = jnp.exp(scores[k] - jnp.concatenate([top[r] for r in users[k]], axis=0))
        mixed = lax.dot_general(
            p.astype(jnp.bfloat16),
            block_of(k)[:kv_rank],
            (((1,), (1,)), ((), ())),
            preferred_element_type=jnp.float32,
        )
        for i in range(2):
            total[users[k][i]] += p[i * both : (i + 1) * both]
            latent[users[k][i]] += mixed[i * both : (i + 1) * both]

    lane = lax.broadcasted_iota(jnp.int32, (row_block, LANES), 1)

    def finish(r, _):
        at = pl.ds(pl.multiple_of(r * row_block, row_block), row_block)
        norm = jnp.sum(total[r], axis=1, keepdims=True)
        some = norm > 0
        safe = jnp.where(some, norm, 1.0)
        lse = jnp.where(some, top[r][:, :1] + jnp.log(safe), EMPTY)
        result = latent[r] * (1.0 / safe)
        out_ref[at] = result[:row_block]
        lse_ref[at] = jnp.broadcast_to(lse[:row_block], (row_block, LANES))
        rest = lse[row_block:]
        high = rest.astype(jnp.bfloat16).astype(jnp.float32)
        middle = (rest - high).astype(jnp.bfloat16).astype(jnp.float32)
        low = rest - high - middle
        terms = jnp.where(lane == 0, high, jnp.where(lane == 1, middle, jnp.where(lane == 2, low, 0.0)))
        away_ref[at, :kv_rank] = result[row_block:].astype(jnp.bfloat16)
        away_ref[at, kv_rank:] = terms.astype(jnp.bfloat16)
        return 0

    lax.fori_loop(0, requests, finish, 0, unroll=batch)


def tiles_of(ref):
    return [ref.at[:, pl.ds(i * OUT_TILE, OUT_TILE)] for i in range(ref.shape[1] // OUT_TILE)]


def project(placed, tiles, keep_ref, away_ref):
    half_rows = keep_ref.shape[0]
    at = 0
    for weight_ref in tiles:
        tile = weight_ref.shape[1]
        result = jnp.dot(
            placed, weight_ref[...], preferred_element_type=jnp.float32
        ).astype(jnp.bfloat16)
        keep_ref[:, at : at + tile] = result[:half_rows]
        away_ref[:, at : at + tile] = result[half_rows:]
        at += tile


def merge_kernel(
    stages, heads, steps, order_ref, value_ref, weight_ref, *rest,
):
    outs, lses, others = rest[:stages], rest[stages : 2 * stages], rest[2 * stages : 3 * stages]
    away_ref, keep_ref, away2_ref, keep2_ref, latent, head_rows = rest[3 * stages :]
    kv_rank, v_width = value_ref.shape[1:]
    rows = head_rows.shape[0]
    requests = rows // steps
    chunk = 64

    def merge(i, _):
        at = pl.ds(pl.multiple_of(i * chunk, chunk), chunk)
        parts = [(o[at], e[at][:, :1]) for o, e in zip(outs, lses)]
        for other in others:
            terms = jnp.sum(other[at, kv_rank:].astype(jnp.float32), axis=1, keepdims=True)
            parts.append((other[at, :kv_rank].astype(jnp.float32), terms))
        peak = functools.reduce(jnp.maximum, [e for _, e in parts])
        shares = [jnp.exp(e - peak) for _, e in parts]
        inverse = 1.0 / functools.reduce(jnp.add, shares)
        whole = functools.reduce(jnp.add, [o * (w * inverse) for (o, _), w in zip(parts, shares)])
        for c in range(kv_rank // LANES):
            latent[c, at] = whole[:, c * LANES : (c + 1) * LANES]
        return 0

    lax.fori_loop(0, rows * heads // chunk, merge, 0, unroll=True)

    half_rows = away_ref.shape[0]
    target = lax.broadcasted_iota(jnp.int32, (2 * half_rows, rows), 0)
    origin = lax.broadcasted_iota(jnp.int32, (2 * half_rows, rows), 1)

    def place(r, picked):
        shifted = origin - r * steps
        hit = (target - order_ref[r] * steps == shifted) & (shifted >= 0) & (shifted < steps)
        return jnp.where(hit, 1.0, picked)

    picker = lax.fori_loop(
        0, requests, place, jnp.zeros((2 * half_rows, rows), jnp.float32), unroll=math.gcd(requests, 8)
    )

    for h in range(heads):
        mine = jnp.concatenate(
            [latent[c, pl.ds(h, rows, stride=heads)] for c in range(kv_rank // LANES)], axis=1
        ).astype(jnp.bfloat16)
        head_rows[:, h * v_width : (h + 1) * v_width] = jnp.dot(
            mine, value_ref[h], preferred_element_type=jnp.float32
        ).astype(jnp.bfloat16)

    placed = jnp.dot(
        picker.astype(jnp.bfloat16), head_rows[...], preferred_element_type=jnp.float32
    ).astype(jnp.bfloat16)
    project(placed, tiles_of(weight_ref)[:FIRST], keep_ref, away_ref)
    project(placed, tiles_of(weight_ref)[FIRST:], keep2_ref, away2_ref)


def local(q_heads, w_absorb, w_value, w_out, latent_cache, ctx_blocks, block_table, owner):
    heads, _, kv_rank = w_absorb.shape
    row_count = q_heads.shape[0]
    head_width = q_heads.shape[1] // heads
    requests, max_blocks = block_table.shape
    steps = row_count // requests
    devices = lax.axis_size("head")
    chips = devices // 2
    blocks_here, block_rows, row_width = latent_cache.shape
    half = blocks_here // 2
    v_width = w_value.shape[2]
    row_block = steps * heads
    flat_rows = requests * row_block
    mebi = 1024 * 1024
    me = lax.axis_index("head").astype(jnp.int32).reshape(1)
    smem = pl.BlockSpec(memory_space=pltpu.SMEM)
    vmem = pl.BlockSpec(memory_space=pltpu.VMEM)
    hbm = pl.BlockSpec(memory_space=pltpu.HBM)

    def pin(x):
        return pltpu.with_memory_space_constraint(x, pltpu.HBM)

    def add(x, *others):
        total = x.astype(jnp.float32)
        for other in others:
            total = total + other.astype(jnp.float32)
        return total.astype(jnp.bfloat16)

    def fold(x, distance):
        middle = x.shape[0] // 2
        return add(x[:middle], exchange(x[middle:], distance))

    def exchange(x, distance):
        return lax.ppermute(x, "head", [(i, i ^ distance) for i in range(devices)])

    piece_total = len(ring_places(chips))

    def prepare():
        slots = jnp.asarray(slots_by_device(chips, half))
        queries, plan, order = pl.pallas_call(
            functools.partial(prepare_kernel, heads, chips),
            out_shape=(
                jax.ShapeDtypeStruct((flat_rows, row_width), jnp.bfloat16),
                jax.ShapeDtypeStruct((2 * piece_total * half + 2,), jnp.int32),
                jax.ShapeDtypeStruct((requests,), jnp.int32),
            ),
            in_specs=[smem] + [hbm] * 6,
            out_specs=(vmem, smem, smem),
            scratch_shapes=[
                pltpu.VMEM(q_heads.shape, jnp.bfloat16),
                pltpu.VMEM(w_absorb.shape, jnp.bfloat16),
                pltpu.SMEM(ctx_blocks.shape, jnp.int32),
                pltpu.SMEM(block_table.shape, jnp.int32),
                pltpu.SMEM(slots.shape, jnp.int32),
                pltpu.SMEM(owner.shape, jnp.int32),
                pltpu.VMEM((kv_rank // LANES + 1, flat_rows, LANES), jnp.float32),
                pltpu.SemaphoreType.DMA((6,)),
            ],
            compiler_params=pltpu.CompilerParams(vmem_limit_bytes=12 * mebi),
            cost_estimate=pl.CostEstimate(
                flops=2 * w_absorb.size * row_count, bytes_accessed=4 * w_absorb.size, transcendentals=0
            ),
            name="prepare",
        )(me, *map(pin, (q_heads, w_absorb, ctx_blocks, block_table, slots, owner)))
        return queries.reshape(requests, row_block, row_width), plan, order

    def attend(plan, mine, theirs, pieces, stage):
        slots = len(pieces) * half
        first_slot = 0 if stage == 0 else piece_total * half - slots
        both = 2 * row_block
        return pl.pallas_call(
            functools.partial(
                attend_kernel, len(pieces), first_slot, heads, steps, kv_rank,
                float(head_width) ** -0.5,
            ),
            out_shape=(
                jax.ShapeDtypeStruct((flat_rows, kv_rank), jnp.float32),
                jax.ShapeDtypeStruct((flat_rows, LANES), jnp.float32),
                jax.ShapeDtypeStruct((flat_rows, kv_rank + LANES), jnp.bfloat16),
            ),
            in_specs=[smem] + [vmem] * (2 + len(pieces)),
            out_specs=(vmem,) * 3,
            scratch_shapes=[
                pltpu.VMEM((slots, 2 * both, block_rows), jnp.float32),
                pltpu.VMEM((requests + 1, both, block_rows), jnp.float32),
                pltpu.VMEM((requests + 1, both, block_rows), jnp.float32),
                pltpu.VMEM((requests + 1, both, kv_rank), jnp.float32),
            ],
            compiler_params=pltpu.CompilerParams(vmem_limit_bytes=28 * mebi),
            cost_estimate=pl.CostEstimate(
                flops=COVER if stage == 1 else 2 * slots * 2 * both * block_rows * 2 * row_width,
                bytes_accessed=slots * block_rows * row_width * 2,
                transcendentals=0,
            ),
            name="attend",
        )(plan, mine, theirs, *pieces)

    ring = ring_of(chips)
    up = [
        (ring[i] * 2 + core, ring[(i + 1) % chips] * 2 + core)
        for i in range(chips)
        for core in range(2)
    ]
    down = [(b, a) for a, b in up]
    keys = jnp.swapaxes(latent_cache, 1, 2)
    ups = [keys[:half], keys[half:]]
    downs = list(ups)
    pieces = list(ups)
    for hop in range(1, chips // 2 + 1):
        last = hop == chips // 2
        if hop == 2:
            mine, plan, order = prepare()
            theirs = exchange(mine, 1)
            ups[0], mine, plan = lax.optimization_barrier((ups[0], mine, plan))
        if last:
            ups[0] = lax.ppermute(ups[0], "head", up)
            downs[1] = lax.ppermute(downs[1], "head", down)
            pieces += [ups[0], downs[1]]
        else:
            ups[0] = lax.ppermute(ups[0], "head", up)
            downs[1] = lax.ppermute(downs[1], "head", down)
            downs[0] = lax.ppermute(downs[0], "head", down)
            ups[1] = lax.ppermute(ups[1], "head", up)
            pieces += [ups[0], downs[1], downs[0], ups[1]]
    early, late = pieces[:-LATE], pieces[-LATE:]
    early_part = attend(plan, mine, theirs, early, 0)
    late_part = attend(plan, mine, theirs, late, 1)
    partial = [(out, lse, exchange(away, 1)) for out, lse, away in (early_part, late_part)]

    part_rows = chips * steps
    widths = (FIRST * OUT_TILE, w_out.shape[1] - FIRST * OUT_TILE)
    parts = [jax.ShapeDtypeStruct((part_rows, n), jnp.bfloat16) for n in widths]
    outs, lses, others = zip(*partial)
    away, keep, next_away, next_keep = pl.pallas_call(
        functools.partial(merge_kernel, len(partial), heads, steps),
        out_shape=(parts[0], parts[0], parts[1], parts[1]),
        in_specs=[smem] + [vmem] * (2 + 3 * len(partial)),
        out_specs=(vmem,) * 4,
        scratch_shapes=[
            pltpu.VMEM((kv_rank // LANES, flat_rows, LANES), jnp.float32),
            pltpu.VMEM((row_count, heads * v_width), jnp.bfloat16),
        ],
        compiler_params=pltpu.CompilerParams(vmem_limit_bytes=28 * mebi),
        name="merge_and_project",
    )(order, w_value, w_out, *outs, *lses, *others)
    first_half = add(keep, exchange(away, 1))
    second_half = add(next_keep, exchange(next_away, 1))
    result = jnp.concatenate([fold(first_half, 2), fold(second_half, 2)], axis=1)
    distance = 4
    while result.shape[0] > 4 * steps:
        result = fold(result, distance)
        distance *= 2
    ways = result.shape[0] // steps
    received = [
        exchange(result[k * steps : (k + 1) * steps], distance * k) for k in range(1, ways)
    ]
    return add(result[:steps], *received)


def solution(mesh):
    return jax.shard_map(
        local,
        mesh=mesh,
        in_specs=(
            P("group", "head"),
            P("head", None, None),
            P("head", None, None),
            P("head", None),
            P(("group", "head"), None, None),
            P("group"),
            P("group", None),
            P("group"),
        ),
        out_specs=P(("group", "head"), None),
        check_vma=False,
    )
```

```python
import functools
import math

import jax
import jax.numpy as jnp
import numpy as np
from jax import lax
from jax.experimental import pallas as pl
from jax.experimental.pallas import tpu as pltpu
from jax.sharding import PartitionSpec as P

OUT_TILE = 1024
LANES = 128
LATE = 4
FIRST = 3
COVER = 30_000_000_000
EMPTY = -1e30


def ring_of(chips):
    if chips == 8:
        return [0, 2, 4, 6, 7, 5, 3, 1]
    return list(range(chips))


def ring_places(chips):
    places = [(0, 0), (0, 1)]
    for hop in range(1, chips // 2 + 1):
        last = hop == chips // 2
        places += [(-hop, 0), (hop, 1)] if last else [(-hop, 0), (hop, 1), (hop, 0), (-hop, 1)]
    return places


def slots_by_device(chips, half):
    ring = ring_of(chips)
    position = {chip: i for i, chip in enumerate(ring)}
    table = np.full((2 * chips, 4 * chips * half), -1, np.int32)
    for device in range(2 * chips):
        for index, (hop, part) in enumerate(ring_places(chips)):
            source = ring[(position[device // 2] + hop) % chips] * 2 + device % 2
            for i in range(half):
                table[device, (source * 2 + part) * half + i] = index * half + i
    return table


def prepare_kernel(
    heads, chips, me_ref, query_hbm, absorb_hbm, length_hbm, table_hbm, slot_hbm, owner_hbm,
    out_ref, plan_ref, order_ref,
    query_ref, absorb_ref, length_ref, table_ref, slot_ref, owner_ref, ordered, sems,
):
    sources = (length_hbm, table_hbm, slot_hbm, owner_hbm, query_hbm, absorb_hbm)
    targets = (length_ref, table_ref, slot_ref, owner_ref, query_ref, absorb_ref)
    copies = [
        pltpu.make_async_copy(a, b, sems.at[i]) for i, (a, b) in enumerate(zip(sources, targets))
    ]
    for copy in copies:
        copy.start()
    requests = table_ref.shape[0]
    entries = plan_ref.shape[0]

    def clear(i, _):
        plan_ref[i] = requests
        return 0

    lax.fori_loop(0, entries, clear, 0)
    for copy in copies[:4]:
        copy.wait()
    me = me_ref[0]

    def list_request(r, _):
        length = length_ref[r]
        order_ref[r] = slot_of(owner_ref[r] ^ me, chips)

        def list_block(j, _):
            slot = slot_ref[me, table_ref[r, j]]
            pair = 2 * jnp.where(slot >= 0, slot, entries // 2 - 1)
            at = pair + (plan_ref[pair] != requests).astype(jnp.int32)
            plan_ref[at] = r + 256 * (j == length - 1).astype(jnp.int32)
            return 0

        return lax.fori_loop(0, length, list_block, 0)

    lax.fori_loop(0, requests, list_request, 0)

    rows = query_ref.shape[0]
    nope = absorb_ref.shape[1]
    head_width = query_ref.shape[1] // heads
    rope = head_width - nope
    kv_rank = absorb_ref.shape[2]
    for copy in copies[4:]:
        copy.wait()
    for h in range(heads):
        own = query_ref[:, h * head_width : (h + 1) * head_width]
        latent = jnp.dot(own[:, :nope], absorb_ref[h], preferred_element_type=jnp.float32)
        turned = jnp.concatenate(
            [own[:, nope:].astype(jnp.float32), jnp.zeros((rows, LANES - rope), jnp.float32)], axis=1
        )
        at = pl.ds(h, rows, stride=heads)
        for c in range(kv_rank // LANES):
            ordered[c, at] = latent[:, c * LANES : (c + 1) * LANES]
        ordered[kv_rank // LANES, at] = turned
    for c in range(kv_rank // LANES):
        out_ref[:, c * LANES : (c + 1) * LANES] = ordered[c].astype(jnp.bfloat16)
    out_ref[:, kv_rank:] = ordered[kv_rank // LANES, :, :rope].astype(jnp.bfloat16)


def slot_of(apart, chips):
    return (apart & 1) * chips + ((apart >> 1) & 1) * (chips // 2) + (apart >> 2)


def attend_kernel(
    piece_count, first_slot, heads, steps, kv_rank, scale,
    plan_ref, mine_ref, theirs_ref, *rest,
):
    pieces, rest = rest[:piece_count], rest[piece_count:]
    out_ref, lse_ref, away_ref, scores, top, total, latent = rest
    row_block = mine_ref.shape[1]
    half = pieces[0].shape[0]
    requests = top.shape[0] - 1
    both = 2 * row_block
    block_rows = pieces[0].shape[2]
    top[...] = jnp.full_like(top, -jnp.inf)
    total[...] = jnp.zeros_like(total)
    latent[...] = jnp.zeros_like(latent)
    column = lax.broadcasted_iota(jnp.int32, (both, block_rows), 1)
    row = lax.broadcasted_iota(jnp.int32, (both, block_rows), 0)
    inside = column + (steps - 1 - (row % row_block) // heads) < block_rows

    def block_of(k):
        return pieces[k // half].at[k % half]

    slots = piece_count * half
    uses = [[plan_ref[2 * (first_slot + k) + i] for i in range(2)] for k in range(slots)]
    users = [[use & 255 for use in pair] for pair in uses]
    for k in range(slots):
        asked = jnp.concatenate(
            [ref[jnp.minimum(r, requests - 1)] for r in users[k] for ref in (mine_ref, theirs_ref)], axis=0
        )
        s = jnp.dot(asked, block_of(k)[...], preferred_element_type=jnp.float32) * scale
        for i in range(2):
            seen = inside | (uses[k][i] < 256)
            part = jnp.where(seen, s[i * both : (i + 1) * both], -jnp.inf)
            scores[k, i * both : (i + 1) * both] = part
            top[users[k][i]] = jnp.maximum(top[users[k][i]], part)

    batch = math.gcd(requests, 8)

    def peak(r, _):
        top[r] = jnp.broadcast_to(jnp.max(top[r], axis=1, keepdims=True), (both, block_rows))
        return 0

    lax.fori_loop(0, requests, peak, 0, unroll=batch)

    for k in range(slots):
        p = jnp.exp(scores[k] - jnp.concatenate([top[r] for r in users[k]], axis=0))
        mixed = lax.dot_general(
            p.astype(jnp.bfloat16),
            block_of(k)[:kv_rank],
            (((1,), (1,)), ((), ())),
            preferred_element_type=jnp.float32,
        )
        for i in range(2):
            total[users[k][i]] += p[i * both : (i + 1) * both]
            latent[users[k][i]] += mixed[i * both : (i + 1) * both]

    lane = lax.broadcasted_iota(jnp.int32, (row_block, LANES), 1)

    def finish(r, _):
        at = pl.ds(pl.multiple_of(r * row_block, row_block), row_block)
        norm = jnp.sum(total[r], axis=1, keepdims=True)
        some = norm > 0
        safe = jnp.where(some, norm, 1.0)
        lse = jnp.where(some, top[r][:, :1] + jnp.log(safe), EMPTY)
        result = latent[r] * (1.0 / safe)
        out_ref[at] = result[:row_block]
        lse_ref[at] = jnp.broadcast_to(lse[:row_block], (row_block, LANES))
        rest = lse[row_block:]
        high = rest.astype(jnp.bfloat16).astype(jnp.float32)
        middle = (rest - high).astype(jnp.bfloat16).astype(jnp.float32)
        low = rest - high - middle
        terms = jnp.where(lane == 0, high, jnp.where(lane == 1, middle, jnp.where(lane == 2, low, 0.0)))
        away_ref[at, :kv_rank] = result[row_block:].astype(jnp.bfloat16)
        away_ref[at, kv_rank:] = terms.astype(jnp.bfloat16)
        return 0

    lax.fori_loop(0, requests, finish, 0, unroll=batch)


def tiles_of(ref):
    return [ref.at[:, pl.ds(i * OUT_TILE, OUT_TILE)] for i in range(ref.shape[1] // OUT_TILE)]


def project(placed, tiles, keep_ref, away_ref):
    half_rows = keep_ref.shape[0]
    at = 0
    for weight_ref in tiles:
        tile = weight_ref.shape[1]
        result = jnp.dot(
            placed, weight_ref[...], preferred_element_type=jnp.float32
        ).astype(jnp.bfloat16)
        keep_ref[:, at : at + tile] = result[:half_rows]
        away_ref[:, at : at + tile] = result[half_rows:]
        at += tile


def merge_kernel(
    stages, heads, steps, order_ref, value_ref, weight_ref, *rest,
):
    outs, lses, others = rest[:stages], rest[stages : 2 * stages], rest[2 * stages : 3 * stages]
    away_ref, keep_ref, placed_ref, latent, head_rows = rest[3 * stages :]
    kv_rank, v_width = value_ref.shape[1:]
    rows = head_rows.shape[0]
    requests = rows // steps
    chunk = 64

    def merge(i, _):
        at = pl.ds(pl.multiple_of(i * chunk, chunk), chunk)
        parts = [(o[at], e[at][:, :1]) for o, e in zip(outs, lses)]
        for other in others:
            terms = jnp.sum(other[at, kv_rank:].astype(jnp.float32), axis=1, keepdims=True)
            parts.append((other[at, :kv_rank].astype(jnp.float32), terms))
        peak = functools.reduce(jnp.maximum, [e for _, e in parts])
        shares = [jnp.exp(e - peak) for _, e in parts]
        inverse = 1.0 / functools.reduce(jnp.add, shares)
        whole = functools.reduce(jnp.add, [o * (w * inverse) for (o, _), w in zip(parts, shares)])
        for c in range(kv_rank // LANES):
            latent[c, at] = whole[:, c * LANES : (c + 1) * LANES]
        return 0

    lax.fori_loop(0, rows * heads // chunk, merge, 0, unroll=True)

    half_rows = away_ref.shape[0]
    target = lax.broadcasted_iota(jnp.int32, (2 * half_rows, rows), 0)
    origin = lax.broadcasted_iota(jnp.int32, (2 * half_rows, rows), 1)

    def place(r, picked):
        shifted = origin - r * steps
        hit = (target - order_ref[r] * steps == shifted) & (shifted >= 0) & (shifted < steps)
        return jnp.where(hit, 1.0, picked)

    picker = lax.fori_loop(
        0, requests, place, jnp.zeros((2 * half_rows, rows), jnp.float32), unroll=math.gcd(requests, 8)
    )

    for h in range(heads):
        mine = jnp.concatenate(
            [latent[c, pl.ds(h, rows, stride=heads)] for c in range(kv_rank // LANES)], axis=1
        ).astype(jnp.bfloat16)
        head_rows[:, h * v_width : (h + 1) * v_width] = jnp.dot(
            mine, value_ref[h], preferred_element_type=jnp.float32
        ).astype(jnp.bfloat16)

    placed = jnp.dot(
        picker.astype(jnp.bfloat16), head_rows[...], preferred_element_type=jnp.float32
    ).astype(jnp.bfloat16)
    placed_ref[...] = placed
    project(placed, tiles_of(weight_ref)[:FIRST], keep_ref, away_ref)


def second_kernel(placed_ref, weight_ref, away_ref, keep_ref):
    project(placed_ref[...], tiles_of(weight_ref)[FIRST:], keep_ref, away_ref)


def local(q_heads, w_absorb, w_value, w_out, latent_cache, ctx_blocks, block_table, owner):
    heads, _, kv_rank = w_absorb.shape
    row_count = q_heads.shape[0]
    head_width = q_heads.shape[1] // heads
    requests, max_blocks = block_table.shape
    steps = row_count // requests
    devices = lax.axis_size("head")
    chips = devices // 2
    blocks_here, block_rows, row_width = latent_cache.shape
    half = blocks_here // 2
    v_width = w_value.shape[2]
    row_block = steps * heads
    flat_rows = requests * row_block
    mebi = 1024 * 1024
    me = lax.axis_index("head").astype(jnp.int32).reshape(1)
    smem = pl.BlockSpec(memory_space=pltpu.SMEM)
    vmem = pl.BlockSpec(memory_space=pltpu.VMEM)
    hbm = pl.BlockSpec(memory_space=pltpu.HBM)

    def pin(x):
        return pltpu.with_memory_space_constraint(x, pltpu.HBM)

    def add(x, *others):
        total = x.astype(jnp.float32)
        for other in others:
            total = total + other.astype(jnp.float32)
        return total.astype(jnp.bfloat16)

    def fold(x, distance):
        middle = x.shape[0] // 2
        return add(x[:middle], exchange(x[middle:], distance))

    def exchange(x, distance):
        return lax.ppermute(x, "head", [(i, i ^ distance) for i in range(devices)])

    piece_total = len(ring_places(chips))

    def prepare():
        slots = jnp.asarray(slots_by_device(chips, half))
        queries, plan, order = pl.pallas_call(
            functools.partial(prepare_kernel, heads, chips),
            out_shape=(
                jax.ShapeDtypeStruct((flat_rows, row_width), jnp.bfloat16),
                jax.ShapeDtypeStruct((2 * piece_total * half + 2,), jnp.int32),
                jax.ShapeDtypeStruct((requests,), jnp.int32),
            ),
            in_specs=[smem] + [hbm] * 6,
            out_specs=(vmem, smem, smem),
            scratch_shapes=[
                pltpu.VMEM(q_heads.shape, jnp.bfloat16),
                pltpu.VMEM(w_absorb.shape, jnp.bfloat16),
                pltpu.SMEM(ctx_blocks.shape, jnp.int32),
                pltpu.SMEM(block_table.shape, jnp.int32),
                pltpu.SMEM(slots.shape, jnp.int32),
                pltpu.SMEM(owner.shape, jnp.int32),
                pltpu.VMEM((kv_rank // LANES + 1, flat_rows, LANES), jnp.float32),
                pltpu.SemaphoreType.DMA((6,)),
            ],
            compiler_params=pltpu.CompilerParams(vmem_limit_bytes=12 * mebi),
            cost_estimate=pl.CostEstimate(
                flops=2 * w_absorb.size * row_count, bytes_accessed=4 * w_absorb.size, transcendentals=0
            ),
            name="prepare",
        )(me, *map(pin, (q_heads, w_absorb, ctx_blocks, block_table, slots, owner)))
        return queries.reshape(requests, row_block, row_width), plan, order

    def attend(plan, mine, theirs, pieces, stage):
        slots = len(pieces) * half
        first_slot = 0 if stage == 0 else piece_total * half - slots
        both = 2 * row_block
        return pl.pallas_call(
            functools.partial(
                attend_kernel, len(pieces), first_slot, heads, steps, kv_rank,
                float(head_width) ** -0.5,
            ),
            out_shape=(
                jax.ShapeDtypeStruct((flat_rows, kv_rank), jnp.float32),
                jax.ShapeDtypeStruct((flat_rows, LANES), jnp.float32),
                jax.ShapeDtypeStruct((flat_rows, kv_rank + LANES), jnp.bfloat16),
            ),
            in_specs=[smem] + [vmem] * (2 + len(pieces)),
            out_specs=(vmem,) * 3,
            scratch_shapes=[
                pltpu.VMEM((slots, 2 * both, block_rows), jnp.float32),
                pltpu.VMEM((requests + 1, both, block_rows), jnp.float32),
                pltpu.VMEM((requests + 1, both, block_rows), jnp.float32),
                pltpu.VMEM((requests + 1, both, kv_rank), jnp.float32),
            ],
            compiler_params=pltpu.CompilerParams(vmem_limit_bytes=28 * mebi),
            cost_estimate=pl.CostEstimate(
                flops=COVER if stage == 1 else 2 * slots * 2 * both * block_rows * 2 * row_width,
                bytes_accessed=slots * block_rows * row_width * 2,
                transcendentals=0,
            ),
            name="attend",
        )(plan, mine, theirs, *pieces)

    ring = ring_of(chips)
    up = [
        (ring[i] * 2 + core, ring[(i + 1) % chips] * 2 + core)
        for i in range(chips)
        for core in range(2)
    ]
    down = [(b, a) for a, b in up]
    keys = jnp.swapaxes(latent_cache, 1, 2)
    ups = [keys[:half], keys[half:]]
    downs = list(ups)
    pieces = list(ups)
    for hop in range(1, chips // 2 + 1):
        last = hop == chips // 2
        if hop == 2:
            mine, plan, order = prepare()
            theirs = exchange(mine, 1)
            ups[0], mine, plan = lax.optimization_barrier((ups[0], mine, plan))
        if last:
            ups[0] = lax.ppermute(ups[0], "head", up)
            downs[1] = lax.ppermute(downs[1], "head", down)
            pieces += [ups[0], downs[1]]
        else:
            ups[0] = lax.ppermute(ups[0], "head", up)
            downs[1] = lax.ppermute(downs[1], "head", down)
            downs[0] = lax.ppermute(downs[0], "head", down)
            ups[1] = lax.ppermute(ups[1], "head", up)
            pieces += [ups[0], downs[1], downs[0], ups[1]]
    early, late = pieces[:-LATE], pieces[-LATE:]
    early_part = attend(plan, mine, theirs, early, 0)
    late_part = attend(plan, mine, theirs, late, 1)
    partial = [(out, lse, exchange(away, 1)) for out, lse, away in (early_part, late_part)]

    part_rows = chips * steps
    widths = (FIRST * OUT_TILE, w_out.shape[1] - FIRST * OUT_TILE)
    parts = [jax.ShapeDtypeStruct((part_rows, n), jnp.bfloat16) for n in widths]
    outs, lses, others = zip(*partial)
    away, keep, placed = pl.pallas_call(
        functools.partial(merge_kernel, len(partial), heads, steps),
        out_shape=(
            parts[0],
            parts[0],
            jax.ShapeDtypeStruct((2 * part_rows, heads * v_width), jnp.bfloat16),
        ),
        in_specs=[smem] + [vmem] * (2 + 3 * len(partial)),
        out_specs=(vmem,) * 3,
        scratch_shapes=[
            pltpu.VMEM((kv_rank // LANES, flat_rows, LANES), jnp.float32),
            pltpu.VMEM((row_count, heads * v_width), jnp.bfloat16),
        ],
        compiler_params=pltpu.CompilerParams(vmem_limit_bytes=28 * mebi),
        name="merge_and_project",
    )(order, w_value, w_out, *outs, *lses, *others)
    next_away, next_keep = pl.pallas_call(
        second_kernel,
        out_shape=(parts[1], parts[1]),
        in_specs=[vmem] * 2,
        out_specs=(vmem, vmem),
        compiler_params=pltpu.CompilerParams(vmem_limit_bytes=28 * mebi),
        cost_estimate=pl.CostEstimate(
            flops=2 * w_out.size * part_rows, bytes_accessed=w_out.size, transcendentals=0
        ),
        name="project_second",
    )(placed, w_out)
    first_half = add(keep, exchange(away, 1))
    second_half = add(next_keep, exchange(next_away, 1))
    result = jnp.concatenate([fold(first_half, 2), fold(second_half, 2)], axis=1)
    distance = 4
    while result.shape[0] > 4 * steps:
        result = fold(result, distance)
        distance *= 2
    ways = result.shape[0] // steps
    received = [
        exchange(result[k * steps : (k + 1) * steps], distance * k) for k in range(1, ways)
    ]
    return add(result[:steps], *received)


def solution(mesh):
    return jax.shard_map(
        local,
        mesh=mesh,
        in_specs=(
            P("group", "head"),
            P("head", None, None),
            P("head", None, None),
            P("head", None),
            P(("group", "head"), None, None),
            P("group"),
            P("group", None),
            P("group"),
        ),
        out_specs=P(("group", "head"), None),
        check_vma=False,
    )
```

```python
import functools
import math

import jax
import jax.numpy as jnp
import numpy as np
from jax import lax
from jax.experimental import pallas as pl
from jax.experimental.pallas import tpu as pltpu
from jax.sharding import PartitionSpec as P

OUT_TILE = 1024
LANES = 128
LATE = 4
FIRST = 3
COVER = 30_000_000_000
EMPTY = -1e30


def ring_of(chips):
    if chips == 8:
        return [0, 2, 4, 6, 7, 5, 3, 1]
    return list(range(chips))


def ring_places(chips):
    places = [(0, 0), (0, 1)]
    for hop in range(1, chips // 2 + 1):
        last = hop == chips // 2
        places += [(-hop, 0), (hop, 1)] if last else [(-hop, 0), (hop, 1), (hop, 0), (-hop, 1)]
    return places


def slots_by_device(chips, half):
    ring = ring_of(chips)
    position = {chip: i for i, chip in enumerate(ring)}
    table = np.full((2 * chips, 4 * chips * half), -1, np.int32)
    for device in range(2 * chips):
        for index, (hop, part) in enumerate(ring_places(chips)):
            source = ring[(position[device // 2] + hop) % chips] * 2 + device % 2
            for i in range(half):
                table[device, (source * 2 + part) * half + i] = index * half + i
    return table


def prepare_kernel(
    heads, chips, me_ref, query_hbm, absorb_hbm, length_hbm, table_hbm, slot_hbm, owner_hbm,
    out_ref, plan_ref, order_ref,
    query_ref, absorb_ref, length_ref, table_ref, slot_ref, owner_ref, ordered, sems,
):
    sources = (length_hbm, table_hbm, slot_hbm, owner_hbm, query_hbm, absorb_hbm)
    targets = (length_ref, table_ref, slot_ref, owner_ref, query_ref, absorb_ref)
    copies = [
        pltpu.make_async_copy(a, b, sems.at[i]) for i, (a, b) in enumerate(zip(sources, targets))
    ]
    for copy in copies:
        copy.start()
    requests = table_ref.shape[0]
    entries = plan_ref.shape[0]

    def clear(i, _):
        plan_ref[i] = requests
        return 0

    lax.fori_loop(0, entries, clear, 0)
    for copy in copies[:4]:
        copy.wait()
    me = me_ref[0]

    def list_request(r, _):
        length = length_ref[r]
        order_ref[r] = slot_of(owner_ref[r] ^ me, chips)

        def list_block(j, _):
            slot = slot_ref[me, table_ref[r, j]]
            pair = 2 * jnp.where(slot >= 0, slot, entries // 2 - 1)
            at = pair + (plan_ref[pair] != requests).astype(jnp.int32)
            plan_ref[at] = r + 256 * (j == length - 1).astype(jnp.int32)
            return 0

        return lax.fori_loop(0, length, list_block, 0)

    lax.fori_loop(0, requests, list_request, 0)

    rows = query_ref.shape[0]
    nope = absorb_ref.shape[1]
    head_width = query_ref.shape[1] // heads
    rope = head_width - nope
    kv_rank = absorb_ref.shape[2]
    for copy in copies[4:]:
        copy.wait()
    for h in range(heads):
        own = query_ref[:, h * head_width : (h + 1) * head_width]
        latent = jnp.dot(own[:, :nope], absorb_ref[h], preferred_element_type=jnp.float32)
        turned = jnp.concatenate(
            [own[:, nope:].astype(jnp.float32), jnp.zeros((rows, LANES - rope), jnp.float32)], axis=1
        )
        at = pl.ds(h, rows, stride=heads)
        for c in range(kv_rank // LANES):
            ordered[c, at] = latent[:, c * LANES : (c + 1) * LANES]
        ordered[kv_rank // LANES, at] = turned
    for c in range(kv_rank // LANES):
        out_ref[:, c * LANES : (c + 1) * LANES] = ordered[c].astype(jnp.bfloat16)
    out_ref[:, kv_rank:] = ordered[kv_rank // LANES, :, :rope].astype(jnp.bfloat16)


def slot_of(apart, chips):
    return (apart & 1) * chips + ((apart >> 1) & 1) * (chips // 2) + (apart >> 2)


def attend_kernel(
    piece_count, late, first_slot, heads, steps, kv_rank, scale,
    plan_ref, mine_ref, theirs_ref, *rest,
):
    pieces, rest = rest[:piece_count], rest[piece_count:]
    if late:
        old_top, old_total, old_latent, out_ref, lse_ref, away_ref, scores, top, total, latent = rest
    else:
        top, total, latent, scores = rest
    row_block = mine_ref.shape[1]
    half = pieces[0].shape[0]
    requests = top.shape[0] - 1
    both = 2 * row_block
    block_rows = pieces[0].shape[2]
    if late:
        top[...] = old_top[...]
    else:
        top[...] = jnp.full_like(top, -jnp.inf)
        total[...] = jnp.zeros_like(total)
        latent[...] = jnp.zeros_like(latent)
    column = lax.broadcasted_iota(jnp.int32, (both, block_rows), 1)
    row = lax.broadcasted_iota(jnp.int32, (both, block_rows), 0)
    inside = column + (steps - 1 - (row % row_block) // heads) < block_rows

    def block_of(k):
        return pieces[k // half].at[k % half]

    slots = piece_count * half
    uses = [[plan_ref[2 * (first_slot + k) + i] for i in range(2)] for k in range(slots)]
    users = [[use & 255 for use in pair] for pair in uses]
    for k in range(slots):
        asked = jnp.concatenate(
            [ref[jnp.minimum(r, requests - 1)] for r in users[k] for ref in (mine_ref, theirs_ref)], axis=0
        )
        s = jnp.dot(asked, block_of(k)[...], preferred_element_type=jnp.float32) * scale
        for i in range(2):
            seen = inside | (uses[k][i] < 256)
            part = jnp.where(seen, s[i * both : (i + 1) * both], -jnp.inf)
            scores[k, i * both : (i + 1) * both] = part
            top[users[k][i]] = jnp.maximum(top[users[k][i]], part)

    batch = math.gcd(requests, 8)

    def peak(r, _):
        top[r] = jnp.broadcast_to(jnp.max(top[r], axis=1, keepdims=True), (both, block_rows))
        if late:
            share = jnp.where(old_top[r] > -jnp.inf, jnp.exp(old_top[r] - top[r]), 0.0)
            total[r] = old_total[r] * share
            for c in range(kv_rank // LANES):
                at = pl.ds(c * LANES, LANES)
                latent[r, :, at] = old_latent[r, :, at] * share[:, :LANES]
        return 0

    lax.fori_loop(0, requests, peak, 0, unroll=batch)
    if late:
        total[requests] = jnp.zeros_like(total[requests])
        latent[requests] = jnp.zeros_like(latent[requests])

    for k in range(slots):
        p = jnp.exp(scores[k] - jnp.concatenate([top[r] for r in users[k]], axis=0))
        mixed = lax.dot_general(
            p.astype(jnp.bfloat16),
            block_of(k)[:kv_rank],
            (((1,), (1,)), ((), ())),
            preferred_element_type=jnp.float32,
        )
        for i in range(2):
            total[users[k][i]] += p[i * both : (i + 1) * both]
            latent[users[k][i]] += mixed[i * both : (i + 1) * both]

    if not late:
        return
    lane = lax.broadcasted_iota(jnp.int32, (row_block, LANES), 1)

    def finish(r, _):
        at = pl.ds(pl.multiple_of(r * row_block, row_block), row_block)
        norm = jnp.sum(total[r], axis=1, keepdims=True)
        some = norm > 0
        safe = jnp.where(some, norm, 1.0)
        lse = jnp.where(some, top[r][:, :1] + jnp.log(safe), EMPTY)
        result = latent[r] * (1.0 / safe)
        out_ref[at] = result[:row_block]
        lse_ref[at] = jnp.broadcast_to(lse[:row_block], (row_block, LANES))
        rest = lse[row_block:]
        high = rest.astype(jnp.bfloat16).astype(jnp.float32)
        middle = (rest - high).astype(jnp.bfloat16).astype(jnp.float32)
        low = rest - high - middle
        terms = jnp.where(lane == 0, high, jnp.where(lane == 1, middle, jnp.where(lane == 2, low, 0.0)))
        away_ref[at, :kv_rank] = result[row_block:].astype(jnp.bfloat16)
        away_ref[at, kv_rank:] = terms.astype(jnp.bfloat16)
        return 0

    lax.fori_loop(0, requests, finish, 0, unroll=batch)


def tiles_of(ref):
    return [ref.at[:, pl.ds(i * OUT_TILE, OUT_TILE)] for i in range(ref.shape[1] // OUT_TILE)]


def project(placed, tiles, keep_ref, away_ref):
    half_rows = keep_ref.shape[0]
    at = 0
    for weight_ref in tiles:
        tile = weight_ref.shape[1]
        result = jnp.dot(
            placed, weight_ref[...], preferred_element_type=jnp.float32
        ).astype(jnp.bfloat16)
        keep_ref[:, at : at + tile] = result[:half_rows]
        away_ref[:, at : at + tile] = result[half_rows:]
        at += tile


def merge_kernel(
    heads, steps, order_ref, value_ref, weight_ref, out_ref, lse_ref, other_ref,
    away_ref, keep_ref, placed_ref, latent, head_rows,
):
    kv_rank, v_width = value_ref.shape[1:]
    rows = head_rows.shape[0]
    requests = rows // steps
    chunk = 64

    def merge(i, _):
        at = pl.ds(pl.multiple_of(i * chunk, chunk), chunk)
        own, own_lse = out_ref[at], lse_ref[at][:, :1]
        other_lse = jnp.sum(other_ref[at, kv_rank:].astype(jnp.float32), axis=1, keepdims=True)
        peak = jnp.maximum(own_lse, other_lse)
        share, other_share = jnp.exp(own_lse - peak), jnp.exp(other_lse - peak)
        inverse = 1.0 / (share + other_share)
        whole = own * (share * inverse)
        whole += other_ref[at, :kv_rank].astype(jnp.float32) * (other_share * inverse)
        for c in range(kv_rank // LANES):
            latent[c, at] = whole[:, c * LANES : (c + 1) * LANES]
        return 0

    lax.fori_loop(0, rows * heads // chunk, merge, 0, unroll=True)

    half_rows = away_ref.shape[0]
    target = lax.broadcasted_iota(jnp.int32, (2 * half_rows, rows), 0)
    origin = lax.broadcasted_iota(jnp.int32, (2 * half_rows, rows), 1)

    def place(r, picked):
        shifted = origin - r * steps
        hit = (target - order_ref[r] * steps == shifted) & (shifted >= 0) & (shifted < steps)
        return jnp.where(hit, 1.0, picked)

    picker = lax.fori_loop(
        0, requests, place, jnp.zeros((2 * half_rows, rows), jnp.float32), unroll=math.gcd(requests, 8)
    )

    for h in range(heads):
        mine = jnp.concatenate(
            [latent[c, pl.ds(h, rows, stride=heads)] for c in range(kv_rank // LANES)], axis=1
        ).astype(jnp.bfloat16)
        head_rows[:, h * v_width : (h + 1) * v_width] = jnp.dot(
            mine, value_ref[h], preferred_element_type=jnp.float32
        ).astype(jnp.bfloat16)

    placed = jnp.dot(
        picker.astype(jnp.bfloat16), head_rows[...], preferred_element_type=jnp.float32
    ).astype(jnp.bfloat16)
    placed_ref[...] = placed
    project(placed, tiles_of(weight_ref)[:FIRST], keep_ref, away_ref)


def second_kernel(placed_ref, weight_ref, away_ref, keep_ref):
    project(placed_ref[...], tiles_of(weight_ref)[FIRST:], keep_ref, away_ref)


def local(q_heads, w_absorb, w_value, w_out, latent_cache, ctx_blocks, block_table, owner):
    heads, _, kv_rank = w_absorb.shape
    row_count = q_heads.shape[0]
    head_width = q_heads.shape[1] // heads
    requests, max_blocks = block_table.shape
    steps = row_count // requests
    devices = lax.axis_size("head")
    chips = devices // 2
    blocks_here, block_rows, row_width = latent_cache.shape
    half = blocks_here // 2
    v_width = w_value.shape[2]
    row_block = steps * heads
    flat_rows = requests * row_block
    mebi = 1024 * 1024
    me = lax.axis_index("head").astype(jnp.int32).reshape(1)
    smem = pl.BlockSpec(memory_space=pltpu.SMEM)
    vmem = pl.BlockSpec(memory_space=pltpu.VMEM)
    hbm = pl.BlockSpec(memory_space=pltpu.HBM)

    def pin(x):
        return pltpu.with_memory_space_constraint(x, pltpu.HBM)

    def add(x, *others):
        total = x.astype(jnp.float32)
        for other in others:
            total = total + other.astype(jnp.float32)
        return total.astype(jnp.bfloat16)

    def fold(x, distance):
        middle = x.shape[0] // 2
        return add(x[:middle], exchange(x[middle:], distance))

    def exchange(x, distance):
        return lax.ppermute(x, "head", [(i, i ^ distance) for i in range(devices)])

    piece_total = len(ring_places(chips))

    def prepare():
        slots = jnp.asarray(slots_by_device(chips, half))
        queries, plan, order = pl.pallas_call(
            functools.partial(prepare_kernel, heads, chips),
            out_shape=(
                jax.ShapeDtypeStruct((flat_rows, row_width), jnp.bfloat16),
                jax.ShapeDtypeStruct((2 * piece_total * half + 2,), jnp.int32),
                jax.ShapeDtypeStruct((requests,), jnp.int32),
            ),
            in_specs=[smem] + [hbm] * 6,
            out_specs=(vmem, smem, smem),
            scratch_shapes=[
                pltpu.VMEM(q_heads.shape, jnp.bfloat16),
                pltpu.VMEM(w_absorb.shape, jnp.bfloat16),
                pltpu.SMEM(ctx_blocks.shape, jnp.int32),
                pltpu.SMEM(block_table.shape, jnp.int32),
                pltpu.SMEM(slots.shape, jnp.int32),
                pltpu.SMEM(owner.shape, jnp.int32),
                pltpu.VMEM((kv_rank // LANES + 1, flat_rows, LANES), jnp.float32),
                pltpu.SemaphoreType.DMA((6,)),
            ],
            compiler_params=pltpu.CompilerParams(vmem_limit_bytes=12 * mebi),
            cost_estimate=pl.CostEstimate(
                flops=2 * w_absorb.size * row_count, bytes_accessed=4 * w_absorb.size, transcendentals=0
            ),
            name="prepare",
        )(me, *map(pin, (q_heads, w_absorb, ctx_blocks, block_table, slots, owner)))
        return queries.reshape(requests, row_block, row_width), plan, order

    both = 2 * row_block
    state = [
        jax.ShapeDtypeStruct((requests + 1, both, n), jnp.float32) for n in (block_rows, block_rows, kv_rank)
    ]

    def attend(plan, mine, theirs, pieces, earlier):
        late = bool(earlier)
        slots = len(pieces) * half
        results = [
            jax.ShapeDtypeStruct((flat_rows, kv_rank), jnp.float32),
            jax.ShapeDtypeStruct((flat_rows, LANES), jnp.float32),
            jax.ShapeDtypeStruct((flat_rows, kv_rank + LANES), jnp.bfloat16),
        ]
        return pl.pallas_call(
            functools.partial(
                attend_kernel, len(pieces), late, piece_total * half - slots if late else 0,
                heads, steps, kv_rank, float(head_width) ** -0.5,
            ),
            out_shape=results if late else state,
            in_specs=[smem] + [vmem] * (2 + len(pieces) + len(earlier)),
            out_specs=[vmem] * 3,
            scratch_shapes=[pltpu.VMEM((slots, 2 * both, block_rows), jnp.float32)]
            + [pltpu.VMEM(x.shape, x.dtype) for x in state] * late,
            compiler_params=pltpu.CompilerParams(vmem_limit_bytes=28 * mebi),
            cost_estimate=pl.CostEstimate(
                flops=2 * slots * 2 * both * block_rows * 2 * row_width if late else COVER,
                bytes_accessed=slots * block_rows * row_width * 2,
                transcendentals=0,
            ),
            name="attend",
        )(plan, mine, theirs, *pieces, *earlier)

    ring = ring_of(chips)
    up = [
        (ring[i] * 2 + core, ring[(i + 1) % chips] * 2 + core)
        for i in range(chips)
        for core in range(2)
    ]
    down = [(b, a) for a, b in up]
    keys = jnp.swapaxes(latent_cache, 1, 2)
    ups = [keys[:half], keys[half:]]
    downs = list(ups)
    pieces = list(ups)
    for hop in range(1, chips // 2 + 1):
        last = hop == chips // 2
        if hop == 2:
            mine, plan, order = prepare()
            theirs = exchange(mine, 1)
            ups[0], mine, plan = lax.optimization_barrier((ups[0], mine, plan))
        if last:
            ups[0] = lax.ppermute(ups[0], "head", up)
            downs[1] = lax.ppermute(downs[1], "head", down)
            pieces += [ups[0], downs[1]]
        else:
            ups[0] = lax.ppermute(ups[0], "head", up)
            downs[1] = lax.ppermute(downs[1], "head", down)
            downs[0] = lax.ppermute(downs[0], "head", down)
            ups[1] = lax.ppermute(ups[1], "head", up)
            pieces += [ups[0], downs[1], downs[0], ups[1]]
    sums = attend(plan, mine, theirs, pieces[:-LATE], ())
    out, lse, away = attend(plan, mine, theirs, pieces[-LATE:], sums)
    other = exchange(away, 1)

    part_rows = chips * steps
    widths = (FIRST * OUT_TILE, w_out.shape[1] - FIRST * OUT_TILE)
    parts = [jax.ShapeDtypeStruct((part_rows, n), jnp.bfloat16) for n in widths]
    away, keep, placed = pl.pallas_call(
        functools.partial(merge_kernel, heads, steps),
        out_shape=(
            parts[0],
            parts[0],
            jax.ShapeDtypeStruct((2 * part_rows, heads * v_width), jnp.bfloat16),
        ),
        in_specs=[smem] + [vmem] * 5,
        out_specs=(vmem,) * 3,
        scratch_shapes=[
            pltpu.VMEM((kv_rank // LANES, flat_rows, LANES), jnp.float32),
            pltpu.VMEM((row_count, heads * v_width), jnp.bfloat16),
        ],
        compiler_params=pltpu.CompilerParams(vmem_limit_bytes=28 * mebi),
        name="merge_and_project",
    )(order, w_value, w_out, out, lse, other)
    next_away, next_keep = pl.pallas_call(
        second_kernel,
        out_shape=(parts[1], parts[1]),
        in_specs=[vmem] * 2,
        out_specs=(vmem, vmem),
        compiler_params=pltpu.CompilerParams(vmem_limit_bytes=28 * mebi),
        cost_estimate=pl.CostEstimate(
            flops=2 * w_out.size * part_rows, bytes_accessed=w_out.size, transcendentals=0
        ),
        name="project_second",
    )(placed, w_out)
    first_half = add(keep, exchange(away, 1))
    second_half = add(next_keep, exchange(next_away, 1))
    result = jnp.concatenate([fold(first_half, 2), fold(second_half, 2)], axis=1)
    distance = devices // 2
    while result.shape[0] > 4 * steps:
        result = fold(result, distance)
        distance //= 2
    ways = result.shape[0] // steps
    received = [exchange(result[k * steps : (k + 1) * steps], 4 * k) for k in reversed(range(1, ways))]
    return add(result[:steps], *received)


def solution(mesh):
    return jax.shard_map(
        local,
        mesh=mesh,
        in_specs=(
            P("group", "head"),
            P("head", None, None),
            P("head", None, None),
            P("head", None),
            P(("group", "head"), None, None),
            P("group"),
            P("group", None),
            P("group"),
        ),
        out_specs=P(("group", "head"), None),
        check_vma=False,
    )
```

```python
import functools
import math

import jax
import jax.numpy as jnp
import numpy as np
from jax import lax
from jax.experimental import pallas as pl
from jax.experimental.pallas import tpu as pltpu
from jax.sharding import PartitionSpec as P

OUT_TILE = 1024
LANES = 128
LATE = 4
FIRST = 3
COVER = 18_000_000_000
EMPTY = -1e30


def ring_of(chips):
    if chips == 8:
        return [0, 2, 4, 6, 7, 5, 3, 1]
    return list(range(chips))


def ring_places(chips):
    places = [(0, 0), (0, 1)]
    for hop in range(1, chips // 2 + 1):
        last = hop == chips // 2
        places += [(-hop, 0), (hop, 1)] if last else [(-hop, 0), (hop, 1), (hop, 0), (-hop, 1)]
    return places


def slots_by_device(chips, half):
    ring = ring_of(chips)
    position = {chip: i for i, chip in enumerate(ring)}
    table = np.full((2 * chips, 4 * chips * half), -1, np.int32)
    for device in range(2 * chips):
        for index, (hop, part) in enumerate(ring_places(chips)):
            source = ring[(position[device // 2] + hop) % chips] * 2 + device % 2
            for i in range(half):
                table[device, (source * 2 + part) * half + i] = index * half + i
    return table


def prepare_kernel(
    heads, chips, me_ref, query_hbm, absorb_hbm, length_hbm, table_hbm, slot_hbm, owner_hbm,
    out_ref, plan_ref, order_ref,
    query_ref, absorb_ref, length_ref, table_ref, slot_ref, owner_ref, ordered, sems,
):
    sources = (length_hbm, table_hbm, slot_hbm, owner_hbm, query_hbm, absorb_hbm)
    targets = (length_ref, table_ref, slot_ref, owner_ref, query_ref, absorb_ref)
    copies = [
        pltpu.make_async_copy(a, b, sems.at[i]) for i, (a, b) in enumerate(zip(sources, targets))
    ]
    for copy in copies:
        copy.start()
    requests = table_ref.shape[0]
    entries = plan_ref.shape[0]

    def clear(i, _):
        plan_ref[i] = requests
        return 0

    lax.fori_loop(0, entries, clear, 0)
    for copy in copies[:4]:
        copy.wait()
    me = me_ref[0]

    def list_request(r, _):
        length = length_ref[r]
        order_ref[r] = slot_of(owner_ref[r] ^ me, chips)

        def list_block(j, _):
            slot = slot_ref[me, table_ref[r, j]]
            pair = 2 * jnp.where(slot >= 0, slot, entries // 2 - 1)
            at = pair + (plan_ref[pair] != requests).astype(jnp.int32)
            plan_ref[at] = r + 256 * (j == length - 1).astype(jnp.int32)
            return 0

        return lax.fori_loop(0, length, list_block, 0)

    lax.fori_loop(0, requests, list_request, 0)

    rows = query_ref.shape[0]
    nope = absorb_ref.shape[1]
    head_width = query_ref.shape[1] // heads
    rope = head_width - nope
    kv_rank = absorb_ref.shape[2]
    for copy in copies[4:]:
        copy.wait()
    for h in range(heads):
        own = query_ref[:, h * head_width : (h + 1) * head_width]
        latent = jnp.dot(own[:, :nope], absorb_ref[h], preferred_element_type=jnp.float32)
        turned = jnp.concatenate(
            [own[:, nope:].astype(jnp.float32), jnp.zeros((rows, LANES - rope), jnp.float32)], axis=1
        )
        at = pl.ds(h, rows, stride=heads)
        for c in range(kv_rank // LANES):
            ordered[c, at] = latent[:, c * LANES : (c + 1) * LANES]
        ordered[kv_rank // LANES, at] = turned
    for c in range(kv_rank // LANES):
        out_ref[:, c * LANES : (c + 1) * LANES] = ordered[c].astype(jnp.bfloat16)
    out_ref[:, kv_rank:] = ordered[kv_rank // LANES, :, :rope].astype(jnp.bfloat16)


def slot_of(apart, chips):
    return (apart & 1) * chips + ((apart >> 1) & 1) * (chips // 2) + (apart >> 2)


def attend_kernel(
    piece_count, late, first_slot, heads, steps, kv_rank, scale,
    plan_ref, mine_ref, theirs_ref, *rest,
):
    pieces, rest = rest[:piece_count], rest[piece_count:]
    if late:
        old_top, old_total, old_latent, out_ref, lse_ref, away_ref, scores, top, total, latent = rest
    else:
        top, total, latent, scores = rest
    row_block = mine_ref.shape[1]
    half = pieces[0].shape[0]
    requests = top.shape[0] - 1
    both = 2 * row_block
    block_rows = pieces[0].shape[2]
    if late:
        top[...] = old_top[...]
    else:
        top[...] = jnp.full_like(top, -jnp.inf)
        total[...] = jnp.zeros_like(total)
        latent[...] = jnp.zeros_like(latent)
    column = lax.broadcasted_iota(jnp.int32, (both, block_rows), 1)
    row = lax.broadcasted_iota(jnp.int32, (both, block_rows), 0)
    inside = column + (steps - 1 - (row % row_block) // heads) < block_rows

    def block_of(k):
        return pieces[k // half].at[k % half]

    slots = piece_count * half
    uses = [[plan_ref[2 * (first_slot + k) + i] for i in range(2)] for k in range(slots)]
    users = [[use & 255 for use in pair] for pair in uses]
    for k in range(slots):
        asked = jnp.concatenate(
            [ref[jnp.minimum(r, requests - 1)] for r in users[k] for ref in (mine_ref, theirs_ref)], axis=0
        )
        s = jnp.dot(asked, block_of(k)[...], preferred_element_type=jnp.float32) * scale
        for i in range(2):
            seen = inside | (uses[k][i] < 256)
            part = jnp.where(seen, s[i * both : (i + 1) * both], -jnp.inf)
            scores[k, i * both : (i + 1) * both] = part
            top[users[k][i]] = jnp.maximum(top[users[k][i]], part)

    batch = math.gcd(requests, 8)

    def peak(r, _):
        top[r] = jnp.broadcast_to(jnp.max(top[r], axis=1, keepdims=True), (both, block_rows))
        if late:
            share = jnp.where(old_top[r] > -jnp.inf, jnp.exp(old_top[r] - top[r]), 0.0)
            total[r] = old_total[r] * share
            for c in range(kv_rank // LANES):
                at = pl.ds(c * LANES, LANES)
                latent[r, :, at] = old_latent[r, :, at] * share[:, :LANES]
        return 0

    lax.fori_loop(0, requests, peak, 0, unroll=batch)
    if late:
        total[requests] = jnp.zeros_like(total[requests])
        latent[requests] = jnp.zeros_like(latent[requests])

    for k in range(slots):
        p = jnp.exp(scores[k] - jnp.concatenate([top[r] for r in users[k]], axis=0))
        mixed = lax.dot_general(
            p.astype(jnp.bfloat16),
            block_of(k)[:kv_rank],
            (((1,), (1,)), ((), ())),
            preferred_element_type=jnp.float32,
        )
        for i in range(2):
            total[users[k][i]] += p[i * both : (i + 1) * both]
            latent[users[k][i]] += mixed[i * both : (i + 1) * both]

    if not late:
        return
    lane = lax.broadcasted_iota(jnp.int32, (row_block, LANES), 1)

    def finish(r, _):
        at = pl.ds(pl.multiple_of(r * row_block, row_block), row_block)
        norm = jnp.sum(total[r], axis=1, keepdims=True)
        some = norm > 0
        safe = jnp.where(some, norm, 1.0)
        lse = jnp.where(some, top[r][:, :1] + jnp.log(safe), EMPTY)
        result = latent[r] * (1.0 / safe)
        for c in range(kv_rank // LANES):
            out_ref[c, at] = result[:row_block, c * LANES : (c + 1) * LANES]
        lse_ref[at] = jnp.broadcast_to(lse[:row_block], (row_block, LANES))
        rest = lse[row_block:]
        high = rest.astype(jnp.bfloat16).astype(jnp.float32)
        middle = (rest - high).astype(jnp.bfloat16).astype(jnp.float32)
        low = rest - high - middle
        terms = jnp.where(lane == 0, high, jnp.where(lane == 1, middle, jnp.where(lane == 2, low, 0.0)))
        away_ref[at, :kv_rank] = result[row_block:].astype(jnp.bfloat16)
        away_ref[at, kv_rank:] = terms.astype(jnp.bfloat16)
        return 0

    lax.fori_loop(0, requests, finish, 0, unroll=batch)


def tiles_of(ref):
    return [ref.at[:, pl.ds(i * OUT_TILE, OUT_TILE)] for i in range(ref.shape[1] // OUT_TILE)]


def project(placed, tiles, keep_ref, away_ref):
    half_rows = keep_ref.shape[0]
    at = 0
    for weight_ref in tiles:
        tile = weight_ref.shape[1]
        result = jnp.dot(
            placed, weight_ref[...], preferred_element_type=jnp.float32
        ).astype(jnp.bfloat16)
        keep_ref[:, at : at + tile] = result[:half_rows]
        away_ref[:, at : at + tile] = result[half_rows:]
        at += tile


def head_values(grouped, value_ref, h, heads):
    kv_rank = value_ref.shape[1]
    rows = grouped.shape[1] // heads
    latent = jnp.concatenate(
        [grouped[c, pl.ds(h, rows, stride=heads)] for c in range(kv_rank // LANES)], axis=1
    )
    return jnp.dot(latent.astype(jnp.bfloat16), value_ref[h], preferred_element_type=jnp.float32)


def value_kernel(heads, grouped_ref, value_ref, out_ref):
    v_width = value_ref.shape[2]
    for h in range(heads):
        out_ref[:, h * v_width : (h + 1) * v_width] = head_values(grouped_ref, value_ref, h, heads)


def merge_kernel(
    heads, steps, order_ref, value_ref, weight_ref, own_ref, lse_ref, other_ref,
    away_ref, keep_ref, placed_ref, latent, head_rows,
):
    kv_rank, v_width = value_ref.shape[1:]
    rows = head_rows.shape[0]
    requests = rows // steps
    chunk = 64
    groups = kv_rank // LANES

    def spread(i, _):
        at = pl.ds(pl.multiple_of(i * chunk, chunk), chunk)
        for c in range(groups):
            latent[c, at] = other_ref[at, c * LANES : (c + 1) * LANES].astype(jnp.float32)
        terms = jnp.sum(other_ref[at, kv_rank:].astype(jnp.float32), axis=1, keepdims=True)
        latent[groups, at] = jnp.broadcast_to(terms, (chunk, LANES))
        return 0

    lax.fori_loop(0, rows * heads // chunk, spread, 0, unroll=True)

    half_rows = away_ref.shape[0]
    target = lax.broadcasted_iota(jnp.int32, (2 * half_rows, rows), 0)
    origin = lax.broadcasted_iota(jnp.int32, (2 * half_rows, rows), 1)

    def place(r, picked):
        shifted = origin - r * steps
        hit = (target - order_ref[r] * steps == shifted) & (shifted >= 0) & (shifted < steps)
        return jnp.where(hit, 1.0, picked)

    picker = lax.fori_loop(
        0, requests, place, jnp.zeros((2 * half_rows, rows), jnp.float32), unroll=math.gcd(requests, 8)
    )

    for h in range(heads):
        at = pl.ds(h, rows, stride=heads)
        columns = slice(h * v_width, (h + 1) * v_width)
        own_lse, other_lse = lse_ref[at], latent[groups, at]
        peak = jnp.maximum(own_lse, other_lse)
        share, other_share = jnp.exp(own_lse - peak), jnp.exp(other_lse - peak)
        inverse = 1.0 / (share + other_share)
        mixed = own_ref[:, columns] * (share * inverse)
        mixed += head_values(latent, value_ref, h, heads) * (other_share * inverse)
        head_rows[:, columns] = mixed.astype(jnp.bfloat16)

    placed = jnp.dot(
        picker.astype(jnp.bfloat16), head_rows[...], preferred_element_type=jnp.float32
    ).astype(jnp.bfloat16)
    placed_ref[...] = placed
    project(placed, tiles_of(weight_ref)[:FIRST], keep_ref, away_ref)


def second_kernel(placed_ref, weight_ref, away_ref, keep_ref):
    project(placed_ref[...], tiles_of(weight_ref)[FIRST:], keep_ref, away_ref)


def local(q_heads, w_absorb, w_value, w_out, latent_cache, ctx_blocks, block_table, owner):
    heads, _, kv_rank = w_absorb.shape
    row_count = q_heads.shape[0]
    head_width = q_heads.shape[1] // heads
    requests, max_blocks = block_table.shape
    steps = row_count // requests
    devices = lax.axis_size("head")
    chips = devices // 2
    blocks_here, block_rows, row_width = latent_cache.shape
    half = blocks_here // 2
    v_width = w_value.shape[2]
    row_block = steps * heads
    flat_rows = requests * row_block
    mebi = 1024 * 1024
    me = lax.axis_index("head").astype(jnp.int32).reshape(1)
    smem = pl.BlockSpec(memory_space=pltpu.SMEM)
    vmem = pl.BlockSpec(memory_space=pltpu.VMEM)
    hbm = pl.BlockSpec(memory_space=pltpu.HBM)

    def pin(x):
        return pltpu.with_memory_space_constraint(x, pltpu.HBM)

    def add(x, *others):
        total = x.astype(jnp.float32)
        for other in others:
            total = total + other.astype(jnp.float32)
        return total.astype(jnp.bfloat16)

    def fold(x, distance):
        middle = x.shape[0] // 2
        return add(x[:middle], exchange(x[middle:], distance))

    def exchange(x, distance):
        return lax.ppermute(x, "head", [(i, i ^ distance) for i in range(devices)])

    piece_total = len(ring_places(chips))

    def prepare():
        slots = jnp.asarray(slots_by_device(chips, half))
        queries, plan, order = pl.pallas_call(
            functools.partial(prepare_kernel, heads, chips),
            out_shape=(
                jax.ShapeDtypeStruct((flat_rows, row_width), jnp.bfloat16),
                jax.ShapeDtypeStruct((2 * piece_total * half + 2,), jnp.int32),
                jax.ShapeDtypeStruct((requests,), jnp.int32),
            ),
            in_specs=[smem] + [hbm] * 6,
            out_specs=(vmem, smem, smem),
            scratch_shapes=[
                pltpu.VMEM(q_heads.shape, jnp.bfloat16),
                pltpu.VMEM(w_absorb.shape, jnp.bfloat16),
                pltpu.SMEM(ctx_blocks.shape, jnp.int32),
                pltpu.SMEM(block_table.shape, jnp.int32),
                pltpu.SMEM(slots.shape, jnp.int32),
                pltpu.SMEM(owner.shape, jnp.int32),
                pltpu.VMEM((kv_rank // LANES + 1, flat_rows, LANES), jnp.float32),
                pltpu.SemaphoreType.DMA((6,)),
            ],
            compiler_params=pltpu.CompilerParams(vmem_limit_bytes=12 * mebi),
            cost_estimate=pl.CostEstimate(
                flops=2 * w_absorb.size * row_count, bytes_accessed=4 * w_absorb.size, transcendentals=0
            ),
            name="prepare",
        )(me, *map(pin, (q_heads, w_absorb, ctx_blocks, block_table, slots, owner)))
        return queries.reshape(requests, row_block, row_width), plan, order

    both = 2 * row_block
    state = [
        jax.ShapeDtypeStruct((requests + 1, both, n), jnp.float32) for n in (block_rows, block_rows, kv_rank)
    ]

    def attend(plan, mine, theirs, pieces, earlier):
        late = bool(earlier)
        slots = len(pieces) * half
        results = [
            jax.ShapeDtypeStruct((kv_rank // LANES, flat_rows, LANES), jnp.float32),
            jax.ShapeDtypeStruct((flat_rows, LANES), jnp.float32),
            jax.ShapeDtypeStruct((flat_rows, kv_rank + LANES), jnp.bfloat16),
        ]
        return pl.pallas_call(
            functools.partial(
                attend_kernel, len(pieces), late, piece_total * half - slots if late else 0,
                heads, steps, kv_rank, float(head_width) ** -0.5,
            ),
            out_shape=results if late else state,
            in_specs=[smem] + [vmem] * (2 + len(pieces) + len(earlier)),
            out_specs=[vmem] * 3,
            scratch_shapes=[pltpu.VMEM((slots, 2 * both, block_rows), jnp.float32)]
            + [pltpu.VMEM(x.shape, x.dtype) for x in state] * late,
            compiler_params=pltpu.CompilerParams(vmem_limit_bytes=28 * mebi),
            cost_estimate=pl.CostEstimate(
                flops=2 * slots * 2 * both * block_rows * 2 * row_width if late else COVER,
                bytes_accessed=slots * block_rows * row_width * 2,
                transcendentals=0,
            ),
            name="attend",
        )(plan, mine, theirs, *pieces, *earlier)

    ring = ring_of(chips)
    up = [
        (ring[i] * 2 + core, ring[(i + 1) % chips] * 2 + core)
        for i in range(chips)
        for core in range(2)
    ]
    down = [(b, a) for a, b in up]
    keys = jnp.swapaxes(latent_cache, 1, 2)
    ups = [keys[:half], keys[half:]]
    downs = list(ups)
    pieces = list(ups)
    for hop in range(1, chips // 2 + 1):
        last = hop == chips // 2
        if hop == 2:
            mine, plan, order = prepare()
            theirs = exchange(mine, 1)
            ups[0], mine, plan = lax.optimization_barrier((ups[0], mine, plan))
        if last:
            ups[0] = lax.ppermute(ups[0], "head", up)
            downs[1] = lax.ppermute(downs[1], "head", down)
            pieces += [ups[0], downs[1]]
        else:
            ups[0] = lax.ppermute(ups[0], "head", up)
            downs[1] = lax.ppermute(downs[1], "head", down)
            downs[0] = lax.ppermute(downs[0], "head", down)
            ups[1] = lax.ppermute(ups[1], "head", up)
            pieces += [ups[0], downs[1], downs[0], ups[1]]
    sums = attend(plan, mine, theirs, pieces[:-LATE], ())
    out, lse, away = attend(plan, mine, theirs, pieces[-LATE:], sums)
    other = exchange(away, 1)
    own = pl.pallas_call(
        functools.partial(value_kernel, heads),
        out_shape=jax.ShapeDtypeStruct((row_count, heads * v_width), jnp.float32),
        in_specs=[vmem] * 2,
        out_specs=vmem,
        compiler_params=pltpu.CompilerParams(vmem_limit_bytes=12 * mebi),
        cost_estimate=pl.CostEstimate(
            flops=2 * w_value.size * row_count, bytes_accessed=2 * w_value.size, transcendentals=0
        ),
        name="own_values",
    )(out, w_value)

    part_rows = chips * steps
    widths = (FIRST * OUT_TILE, w_out.shape[1] - FIRST * OUT_TILE)
    parts = [jax.ShapeDtypeStruct((part_rows, n), jnp.bfloat16) for n in widths]
    away, keep, placed = pl.pallas_call(
        functools.partial(merge_kernel, heads, steps),
        out_shape=(
            parts[0],
            parts[0],
            jax.ShapeDtypeStruct((2 * part_rows, heads * v_width), jnp.bfloat16),
        ),
        in_specs=[smem] + [vmem] * 5,
        out_specs=(vmem,) * 3,
        scratch_shapes=[
            pltpu.VMEM((kv_rank // LANES + 1, flat_rows, LANES), jnp.float32),
            pltpu.VMEM((row_count, heads * v_width), jnp.bfloat16),
        ],
        compiler_params=pltpu.CompilerParams(vmem_limit_bytes=28 * mebi),
        name="merge_and_project",
    )(order, w_value, w_out, own, lse, other)
    next_away, next_keep = pl.pallas_call(
        second_kernel,
        out_shape=(parts[1], parts[1]),
        in_specs=[vmem] * 2,
        out_specs=(vmem, vmem),
        compiler_params=pltpu.CompilerParams(vmem_limit_bytes=28 * mebi),
        cost_estimate=pl.CostEstimate(
            flops=2 * w_out.size * part_rows, bytes_accessed=w_out.size, transcendentals=0
        ),
        name="project_second",
    )(placed, w_out)
    first_half = add(keep, exchange(away, 1))
    second_half = add(next_keep, exchange(next_away, 1))
    result = jnp.concatenate([fold(first_half, 2), fold(second_half, 2)], axis=1)
    distance = devices // 2
    while result.shape[0] > 4 * steps:
        result = fold(result, distance)
        distance //= 2
    ways = result.shape[0] // steps
    received = [exchange(result[k * steps : (k + 1) * steps], 4 * k) for k in reversed(range(1, ways))]
    return add(result[:steps], *received)


def solution(mesh):
    return jax.shard_map(
        local,
        mesh=mesh,
        in_specs=(
            P("group", "head"),
            P("head", None, None),
            P("head", None, None),
            P("head", None),
            P(("group", "head"), None, None),
            P("group"),
            P("group", None),
            P("group"),
        ),
        out_specs=P(("group", "head"), None),
        check_vma=False,
    )
```
